512 devices in a mesh: blk: 8 (over y, x_hi), grp: 64 (over z, x_lo, core).
Axes of the slice: x: 4 (x_hi: 2, x_lo: 2; x = x_hi * 2 + x_lo), y: 4, z: 16, core: 2. Of those that a mesh axis runs over, the one named last changes fastest.
Arguments:
- positions: float32 [3, 131072], P(None, ('blk', 'grp')), may hold values from -6 to 6
- velocities: float32 [3, 131072], P(None, ('blk', 'grp')), may hold values from -6 to 6
- accelerations: float32 [3, 131072], P(None, ('blk', 'grp')), may hold values from -4 to 4
- jerks: float32 [3, 131072], P(None, ('blk', 'grp')), may hold values from -4 to 4
- mass_weight: float32 [131072], P(('blk', 'grp')), may hold values from 0.3 to 3
- levels: int32 [131072], P(('blk', 'grp')), may hold values from 0 to 3, as said below
- active: int32 [2, 12288], P(None, ('blk', 'grp')), may hold values from 0 to 255, as said below
- counts: int32 [2, 512], P(None, ('blk', 'grp')), may hold values from 1 to 24
Outputs:
- positions_out: float32 [3, 131072], P(None, ('blk', 'grp'))
- velocities_out: float32 [3, 131072], P(None, ('blk', 'grp'))
- accelerations_out: float32 [3, 131072], P(None, ('blk', 'grp'))
- jerks_out: float32 [3, 131072], P(None, ('blk', 'grp'))
- fresh_forces: float32 [2, 6, 12288], P(None, None, ('blk', 'grp'))
The draws below stay inside these ranges and needn't reach their ends.
Inputs may be any that keep to these rules, and one draw needn't show every extreme that they name: `active`: entries are local indices of the owner's particles; the live slots of one owner's list are distinct, dead slots hold 0. `levels`: particles not named in any list have level 2 or 3.
All inputs are finite; a program needn't handle non-finite values.
Results may differ from the reference program's by a relative error of at most 0.0003.
Values sent between devices are 32-bit elements; how exact they have to be, the bound alone decides.
No kernel may reach another device: no remote copies, remote signals or barrier semaphores. Data moves between devices by JAX's collectives and lax.ppermute only.
A program may use at most 64 MiB of HBM per device.

```python
import math
import jax
import jax.numpy as jnp
from jax import lax

PART_DEV = 256
ACT = 24
OWNERS = 512
NPART = 131072


def roster(key):
    load_key, full_key, first_key, order_key, rest_key = jax.random.split(jax.random.fold_in(key, 17), 5)
    owner_ids = jnp.arange(OWNERS, dtype=jnp.int32)
    busiest = jax.random.randint(full_key, (), 0, OWNERS)
    pair_ids = (owner_ids // 2).astype(jnp.int32)
    odd_owner = (owner_ids % 2).astype(jnp.int32)
    pair_draw = jax.random.randint(first_key, (OWNERS // 2,), 1, ACT).astype(jnp.int32)
    pair_slots = jnp.arange(OWNERS // 2, dtype=jnp.int32)
    pair_draw = jnp.where(pair_slots == busiest // 2, ACT - 1, pair_draw).astype(jnp.int32)
    even_first = pair_draw[pair_ids]
    first = jnp.where(odd_owner == 1, ACT - even_first, even_first).astype(jnp.int32)
    load = ACT - jax.random.randint(load_key, (OWNERS,), 0, ACT // 8 + 1)
    load = jnp.where(owner_ids == busiest, ACT, load).astype(jnp.int32)
    load = jnp.maximum(load, first).astype(jnp.int32)
    orders = jax.vmap(lambda k: jax.random.permutation(k, PART_DEV))(jax.random.split(order_key, OWNERS)).astype(jnp.int32)
    rank = jnp.arange(PART_DEV, dtype=jnp.int32)
    slower = 2 + jax.random.randint(rest_key, (OWNERS, PART_DEV), 0, 2)
    by_rank = jnp.where(rank[None, :] < first[:, None], 0, jnp.where(rank[None, :] < load[:, None], 1, slower)).astype(jnp.int32)
    empty = jnp.zeros((OWNERS, PART_DEV), jnp.int32)
    level_rows = jax.vmap(lambda row, order, value: row.at[order].set(value))(empty, orders, by_rank)
    slots = jnp.arange(ACT, dtype=jnp.int32)
    leading = orders[:, :ACT]
    step_one = jnp.where(slots[None, :] < first[:, None], leading, 0)
    step_two = jnp.where(slots[None, :] < load[:, None], leading, 0)
    lists = jnp.stack([step_one, step_two]).reshape(2, OWNERS * ACT).astype(jnp.int32)
    tallies = jnp.stack([first, load]).astype(jnp.int32)
    return (level_rows.reshape(OWNERS * PART_DEV).astype(jnp.int32), lists, tallies)


def draw_levels(key, part):
    return roster(key)[0]


def draw_active(key, part):
    return roster(key)[1]


def draw_counts(key, part):
    return roster(key)[2]


def block_scale(rng, shape, pieces, least, largest):
    loudness = 1.0
    for position, blocks in pieces:
        heights = jax.random.uniform(jax.random.fold_in(jax.random.fold_in(rng, 6), position), (blocks,), jnp.float32, least / len(pieces), largest / len(pieces))
        loudness = loudness * jnp.repeat(jnp.exp(heights), shape[position] // blocks).reshape((-1,) + (1,) * (len(shape) - 1 - position))
    return loudness


def scatter_about(key, extent, scale, most, cuts=(), kind=jnp.bfloat16):
    gain = block_scale(key, extent, cuts, -0.22, 0.18) if cuts else 1.0
    values = jax.random.normal(key, extent, jnp.float32) * scale * gain
    return jnp.minimum(jnp.maximum(values, -most), most).astype(kind)


def setup_inputs(seed: int = 0) -> dict:
    key_of = jax.random.split(jax.random.key(seed), 9)
    positions = scatter_about(key_of[0], (3, NPART), 1.0, 6.0, ((1, 512),), jnp.float32)
    velocities = scatter_about(key_of[1], (3, NPART), 1.0, 6.0, ((1, 512),), jnp.float32)
    accelerations = scatter_about(key_of[2], (3, NPART), 0.3, 4.0, ((1, 512),), jnp.float32)
    jerks = scatter_about(key_of[3], (3, NPART), 0.3, 4.0, ((1, 512),), jnp.float32)
    mass_weight = jnp.clip(jnp.exp(math.log(3.0) - 2.3025851 * jax.random.uniform(key_of[4], (NPART,), jnp.float32) ** block_scale(key_of[4], (NPART,), ((0, 512),), -0.2, 0.2)), 0.3, 3.0)
    levels = draw_levels(jax.random.fold_in(key_of[8], 71), 0)
    active = draw_active(jax.random.fold_in(key_of[8], 71), 0)
    counts = draw_counts(jax.random.fold_in(key_of[8], 71), 0)
    return dict(positions=positions, velocities=velocities, accelerations=accelerations, jerks=jerks, mass_weight=mass_weight, levels=levels, active=active, counts=counts)


STEP_BASE = 0.125
SOFTEN = 0.01

def predict(pos, vel, acc, jerk, elapsed):
    pred_pos = pos + elapsed * (vel + elapsed * (acc * 0.5 + elapsed * jerk / 6.0))
    pred_vel = vel + elapsed * (acc + elapsed * jerk * 0.5)
    return (pred_pos, pred_vel)

def correct(pos, vel, acc, jerk, new_acc, new_jerk, stride, hit):
    half = 0.5 * stride
    square = stride * stride / 12.0
    vel_new = vel + half * (acc + new_acc) + square * (jerk - new_jerk)
    pos_new = pos + half * (vel + vel_new) + square * (acc - new_acc)
    return (jnp.where(hit, pos_new, pos), jnp.where(hit, vel_new, vel), jnp.where(hit, new_acc, acc), jnp.where(hit, new_jerk, jerk))

def pair_terms(iblock, jpart):
    dpos = jpart[0:3, :, None] - iblock[0:3, None, :]
    dvel = jpart[3:6, :, None] - iblock[3:6, None, :]
    dist = dpos[0] * dpos[0] + dpos[1] * dpos[1] + dpos[2] * dpos[2] + SOFTEN
    inverse = lax.rsqrt(dist)
    weight = jpart[6][:, None] * inverse * inverse * inverse
    radial = 3.0 * (dpos[0] * dvel[0] + dpos[1] * dvel[1] + dpos[2] * dvel[2]) * inverse * inverse
    accel = lax.optimization_barrier(jnp.sum(weight[None] * dpos, axis=1))
    jerk = lax.optimization_barrier(jnp.sum(weight[None] * (dvel - radial[None] * dpos), axis=1))
    return jnp.concatenate([accel, jerk], axis=0)

def forces_all(chosen, jdata):
    rows = chosen.shape[1]
    width = 64
    blocks = chosen.reshape(6, rows // width, width).transpose(1, 0, 2)
    result = lax.map(lambda iblock: pair_terms(iblock, jdata), blocks)
    return result.transpose(1, 0, 2).reshape(6, rows)

def reference(positions, velocities, accelerations, jerks, mass_weight, levels, active, counts):
    mass = mass_weight / NPART
    clock = jnp.zeros((NPART,), jnp.float32)
    stride = STEP_BASE * jnp.left_shift(jnp.ones_like(levels), levels).astype(jnp.float32)
    slot = jnp.arange(OWNERS * ACT, dtype=jnp.int32)
    owner = (slot // ACT).astype(jnp.int32)
    global_index = (active + owner[None, :] * PART_DEV).astype(jnp.int32)
    pos, vel, acc, jerk = (positions, velocities, accelerations, jerks)
    recorded = []
    for step in range(2):
        now = STEP_BASE * (step + 1)
        elapsed = now - clock
        pred_pos, pred_vel = predict(pos, vel, acc, jerk, elapsed)
        live = slot % ACT < counts[step][owner]
        target = jnp.where(live, global_index[step], NPART).astype(jnp.int32)
        pred_both = jnp.concatenate([pred_pos, pred_vel], axis=0)
        chosen = pred_both[:, jnp.minimum(target, NPART - 1)]
        jdata = jnp.concatenate([pred_pos, pred_vel, mass[None, :]], axis=0)
        fresh = forces_all(chosen, jdata)
        recorded.append(jnp.where(live[None, :], fresh, jnp.zeros_like(fresh)))
        spread = jnp.zeros((6, NPART), jnp.float32).at[:, target].set(fresh, mode='drop')
        hit = jnp.zeros((NPART,), jnp.float32).at[target].set(1.0, mode='drop') > 0.5
        pos, vel, acc, jerk = correct(pos, vel, acc, jerk, spread[0:3], spread[3:6], stride, hit)
        clock = jnp.where(hit, now, clock)
    return (pos, vel, acc, jerk, jnp.stack(recorded))
```

```python
import jax
import jax.numpy as jnp
from jax import lax
from jax.experimental import pallas as pl
from jax.experimental.pallas import tpu as pltpu
from jax.sharding import Mesh, PartitionSpec as P

STEP_BASE = 0.125
SOFTEN = 0.01
PART = 256
SLOTS = 24
CHIPS = 16
PLANE = 2 * CHIPS
COLUMN = 16
COLS = SLOTS * CHIPS
SHARE = SLOTS // 2
LANES = 128
LISTED = 32
RATES = 64
ALL_AXES = ("y", "h", "z", "l", "c")
PLANE_AXES = ("y", "h", "l", "c")
EXACT = lax.Precision.HIGHEST
F32 = jnp.float32
I32 = jnp.int32
NT = (((1,), (1,)), ((), ()))


def predict(pos, vel, acc, jerk, elapsed):
    pred_pos = pos + elapsed * (vel + elapsed * (acc * 0.5 + elapsed * jerk / 6.0))
    pred_vel = vel + elapsed * (acc + elapsed * jerk * 0.5)
    return (pred_pos, pred_vel)


def correct(pos, vel, acc, jerk, new_acc, new_jerk, stride):
    half = 0.5 * stride
    square = stride * stride / 12.0
    vel_new = vel + half * (acc + new_acc) + square * (jerk - new_jerk)
    pos_new = pos + half * (vel + vel_new) + square * (acc - new_acc)
    return (pos_new, vel_new)


def iota(shape, axis):
    return lax.broadcasted_iota(I32, shape, axis)


def prepare_kernel(total, cnt, pos, vel, acc, jerk, weight, levels, active, zsend, isend, place, slots, jrows, srows):
    core = lax.axis_index("c")
    mass = weight[...] / total
    lev = levels[...]
    p, v, a, j = pos[...], vel[...], acc[...], jerk[...]
    p1, v1 = predict(p, v, a, j, STEP_BASE)
    p2, v2 = predict(p, v, a, j, 2 * STEP_BASE)
    jrows[0:3] = p1
    jrows[3:6] = v1
    jrows[6:7] = mass
    jrows[7:8] = jnp.where(lev == 0, 0.0, mass)
    jrows[8:11] = p2
    jrows[11:14] = v2
    jrows[14:16] = jnp.zeros((2, PART), F32)
    rows = jrows[...]
    for k in range(COLUMN):
        zsend[k] = rows
    srows[...] = jnp.zeros(srows.shape, F32)
    srows[0:3] = p
    srows[3:6] = v
    srows[6:7] = mass
    srows[8:11] = p2
    srows[11:14] = v2
    srows[16:19] = a
    srows[19:22] = j

    n1, n2 = cnt[0, 0], cnt[1, 0]
    off0 = jnp.where(core == 1, SLOTS - n1, 0)
    off1 = jnp.where(core == 1, n1, 0)
    who = iota((PART, SLOTS), 0)
    slot = iota((PART, SLOTS), 1)
    a1 = ((who == active[0:1, :]) & (slot < n1)).astype(F32)
    a2 = ((who == active[1:2, :]) & (slot < n2)).astype(F32)
    col = iota((LANES, SLOTS), 0)
    cslot = iota((LANES, SLOTS), 1)
    first = (col == cslot + off0) & (cslot < n1)
    again = (col == cslot + off0 + RATES) & (cslot < n1)
    first_f = first.astype(F32)
    listed = jnp.dot(jnp.broadcast_to(lev.astype(F32), (8, PART)), a2, preferred_element_type=F32)
    live = iota((8, SLOTS), 1) < n2
    is0 = (live & (listed < 0.5)).astype(F32)
    is1 = (live & (listed > 0.5) & (listed < 1.5)).astype(F32)
    before = (iota((SLOTS, SLOTS), 0) < iota((SLOTS, SLOTS), 1)).astype(F32)
    rank0 = jnp.dot(is0, before, preferred_element_type=F32)[0:1].astype(I32)
    rank1 = jnp.dot(is1, before, preferred_element_type=F32)[0:1].astype(I32)
    second = ((col == rank1 + (off1 + LISTED)) & (is1[0:1] > 0.5)).astype(F32)
    held = ((col == rank0 + off0) & (is0[0:1] > 0.5)).astype(F32)
    spots = lax.dot_general(a1, first_f + again.astype(F32), NT, preferred_element_type=F32)
    spots = spots + lax.dot_general(a2, second, NT, preferred_element_type=F32)
    place[...] = spots
    slots[0] = first_f
    slots[1] = held + second
    picked = jnp.dot(srows[...], spots, precision=EXACT, preferred_element_type=F32)
    lane = iota((8, LANES), 1)
    payload = jnp.where(lane < LISTED, picked[0:8], jnp.where(lane < RATES, picked[8:16], picked[16:24]))
    for k in range(PLANE):
        isend[k] = payload


def gather_terms(jt, bases, rows, targets, sums):
    def one(t, sums):
        sums = list(sums)
        tile = jt[pl.ds(pl.multiple_of(t * 8, 8), 8), :]
        for base in bases:
            cols = [jnp.broadcast_to(tile[:, k : k + 1], (8, LANES)) for k in base]
            for i, target in enumerate(targets):
                dx, dy, dz = (cols[k] - target[k] for k in range(3))
                du, dv, dw = (cols[k] - target[k] for k in range(3, 6))
                inv = lax.rsqrt(dx * dx + dy * dy + dz * dz + SOFTEN)
                inv2 = inv * inv
                weight = cols[6] * inv * inv2
                radial = (dx * du + dy * dv + dz * dw) * (inv2 * 3.0)
                ax, ay, az, jx, jy, jz = sums[6 * i : 6 * i + 6]
                sums[6 * i : 6 * i + 6] = (
                    ax + weight * dx,
                    ay + weight * dy,
                    az + weight * dz,
                    jx + weight * (du - radial * dx),
                    jy + weight * (dv - radial * dy),
                    jz + weight * (dw - radial * dz),
                )
        return tuple(sums)

    return lax.fori_loop(0, rows // 8, one, sums)


def tiles_of(states):
    return [
        [jnp.broadcast_to(states[k : k + 1, LANES * t : LANES * (t + 1)], (8, LANES)) for k in range(6)]
        for t in range(states.shape[1] // LANES)
    ]


def zero_sums(count):
    return tuple(jnp.zeros((8, LANES), F32) for _ in range(6 * count))


def store_sums(out, sums):
    out[6:8] = jnp.zeros((2, out.shape[1]), F32)
    for i in range(len(sums) // 6):
        for k in range(6):
            out[k : k + 1, LANES * i : LANES * (i + 1)] = jnp.sum(sums[6 * i + k], axis=0, keepdims=True)


def first_bases():
    return [[16 * s + k for k in range(7)] for s in range(COLUMN)]


def later_bases():
    return [[16 * s + k for k in (8, 9, 10, 11, 12, 13, 7)] for s in range(COLUMN)]


def first_kernel(zrecv, irecv, psend, known, other, jt, part):
    jt[...] = jnp.transpose(zrecv[...].reshape(COLUMN * 16, PART))
    for q in range(CHIPS):
        block = irecv[2 * q] + irecv[2 * q + 1]
        here = slice(SLOTS * q, SLOTS * (q + 1))
        known[0:8, here] = block[:, 0:SLOTS]
        known[8:16, here] = block[:, RATES : RATES + SLOTS]
        other[:, here] = block[:, LISTED : LISTED + SLOTS]
    p1, v1 = predict(known[0:3], known[3:6], known[8:11], known[11:14], STEP_BASE)
    states = jnp.concatenate([p1, v1], axis=0)
    targets = tiles_of(states)
    sums = gather_terms(jt, first_bases(), PART, targets, zero_sums(len(targets)))
    store_sums(part, sums)
    whole = part[...]
    for k in range(PLANE):
        psend[k] = whole


def later_kernel(jt, states, out):
    targets = tiles_of(states[...])
    sums = gather_terms(jt, later_bases(), PART, targets, zero_sums(len(targets)))
    store_sums(out, sums)


def update_kernel(precv, known, zsend, moved, mine):
    total = precv[0]
    for k in range(1, PLANE):
        total = total + precv[k]
    p, v, a, j = known[0:3], known[3:6], known[8:11], known[11:14]
    new_a, new_j = total[0:3], total[3:6]
    pos, vel = correct(p, v, a, j, new_a, new_j, STEP_BASE)
    p2, v2 = predict(pos, vel, new_a, new_j, STEP_BASE)
    moved[0:3] = p2
    moved[3:6] = v2
    moved[6:7] = known[6:7]
    moved[7:8] = jnp.zeros((1, COLS), F32)
    chip = (lax.axis_index("y") * 2 + lax.axis_index("h")) * 2 + lax.axis_index("l")
    core = lax.axis_index("c")
    row = iota((COLS, LANES), 0)
    lane = iota((COLS, LANES), 1)
    share = ((row == lane + (chip * SLOTS + core * SHARE)) & (lane < SHARE)).astype(F32)
    block = ((row == lane + chip * SLOTS) & (lane < SLOTS)).astype(F32)
    payload = jnp.dot(moved[...], share, precision=EXACT, preferred_element_type=F32)
    for k in range(COLUMN):
        zsend[k] = payload
    mine[...] = jnp.dot(total, block, precision=EXACT, preferred_element_type=F32)


def last_kernel(zrecv, moved, other, part0, part1, fsend, jt, sum0, sum1):
    jt[...] = jnp.transpose(zrecv[...].reshape(COLUMN * 8, LANES))
    bases = [[8 * s + k for k in range(7)] for s in range(COLUMN)]
    for states, part, out in ((moved, part0, sum0), (other, part1, sum1)):
        targets = tiles_of(states[...])
        sums = gather_terms(jt, bases, 16, targets, zero_sums(len(targets)))
        store_sums(out, sums)
        out[...] = out[...] + part[...]
    for q in range(CHIPS):
        here = slice(SLOTS * q, SLOTS * (q + 1))
        for k in (2 * q, 2 * q + 1):
            fsend[k] = jnp.zeros((8, LANES), F32)
            fsend[k, :, 0:SLOTS] = sum0[:, here]
            fsend[k, :, LISTED : LISTED + SLOTS] = sum1[:, here]


def finish_kernel(pos, vel, acc, jerk, levels, frecv, mine, place, slots, pos_o, vel_o, acc_o, jerk_o, fresh):
    total = frecv[0]
    for k in range(1, PLANE):
        total = total + frecv[k]
    once = mine[...]
    fresh[0] = jnp.dot(once, slots[0], precision=EXACT, preferred_element_type=F32)[0:6]
    fresh[1] = jnp.dot(total, slots[1], precision=EXACT, preferred_element_type=F32)[0:6]
    lane = iota((8, LANES), 1)
    spots = place[...]
    lev = levels[...]
    stride = STEP_BASE * jnp.left_shift(jnp.ones_like(lev), lev).astype(F32)
    p, v, a, j = pos[...], vel[...], acc[...], jerk[...]
    for step, values in enumerate((once, total)):
        spread = lax.dot_general(jnp.where(lane < RATES, values, 0.0), spots, NT, precision=EXACT, preferred_element_type=F32)
        new_a, new_j = spread[0:3], spread[3:6]
        hit = lev <= step
        p_new, v_new = correct(p, v, a, j, new_a, new_j, stride)
        p, v = jnp.where(hit, p_new, p), jnp.where(hit, v_new, v)
        a, j = jnp.where(hit, new_a, a), jnp.where(hit, new_j, j)
    pos_o[...] = p
    vel_o[...] = v
    acc_o[...] = a
    jerk_o[...] = j


def call(kernel, ins, outs, scratch=(), smem=0, pairs=0):
    vmem = pl.BlockSpec(memory_space=pltpu.VMEM)
    ops = max(pairs * 40, 1000)
    return pl.pallas_call(
        kernel,
        out_shape=[jax.ShapeDtypeStruct(s, F32) for s in outs],
        in_specs=[pl.BlockSpec(memory_space=pltpu.SMEM)] * smem + [vmem] * (len(ins) - smem),
        out_specs=[vmem] * len(outs),
        scratch_shapes=[pltpu.VMEM(s, F32) for s in scratch],
        compiler_params=pltpu.CompilerParams(vmem_limit_bytes=32 * 1024 * 1024),
        cost_estimate=pl.CostEstimate(flops=ops, bytes_accessed=65536, transcendentals=pairs),
    )(*ins)


def exchange(value, axes):
    return lax.all_to_all(value, axes, 0, 0, tiled=True)


def body(positions, velocities, accelerations, jerks, mass_weight, levels, active, counts):
    total_part = PART * lax.axis_size(ALL_AXES)
    lev = levels.reshape(1, PART)
    state = (positions, velocities, accelerations, jerks)

    def prepare(*refs):
        prepare_kernel(total_part, *refs)

    zsend, isend, place, slots = call(
        prepare,
        (counts, *state, mass_weight.reshape(1, PART), lev, active),
        [(COLUMN, 16, PART), (PLANE, 8, LANES), (PART, LANES), (2, LANES, SLOTS)],
        [(16, PART), (24, PART)],
        smem=1,
    )
    irecv = exchange(isend, PLANE_AXES)
    zrecv = exchange(zsend, "z")
    pairs = COLS * PART * COLUMN
    psend, known, other, jt = call(
        first_kernel,
        (zrecv, irecv),
        [(PLANE, 8, COLS), (16, COLS), (8, COLS), (PART, PART)],
        [(8, COLS)],
        pairs=pairs,
    )
    precv = exchange(psend, PLANE_AXES)
    (part1,) = call(later_kernel, (jt, other), [(8, COLS)], pairs=pairs)
    zsend2, moved, mine = call(update_kernel, (precv, known), [(COLUMN, 8, LANES), (8, COLS), (8, LANES)])
    zrecv2 = exchange(zsend2, "z")
    (part0,) = call(later_kernel, (jt, moved), [(8, COLS)], pairs=pairs)
    (fsend,) = call(
        last_kernel,
        (zrecv2, moved, other, part0, part1),
        [(PLANE, 8, LANES)],
        [(LANES, LANES), (8, COLS), (8, COLS)],
    )
    frecv = exchange(fsend, PLANE_AXES)
    return call(
        finish_kernel,
        (*state, lev, frecv, mine, place, slots),
        [(3, PART)] * 4 + [(2, 6, SLOTS)],
    )


def solution(mesh):
    fine = Mesh(mesh.devices.reshape(4, 2, 16, 2, 2), ALL_AXES)
    rows, flat = P(None, ALL_AXES), P(ALL_AXES)
    in_specs = (rows, rows, rows, rows, flat, flat, rows, rows)
    out_specs = (rows, rows, rows, rows, P(None, None, ALL_AXES))
    return jax.shard_map(body, mesh=fine, in_specs=in_specs, out_specs=out_specs, check_vma=False)
```

```python
import jax
import jax.numpy as jnp
from jax import lax
from jax.experimental import pallas as pl
from jax.experimental.pallas import tpu as pltpu
from jax.sharding import Mesh, PartitionSpec as P

STEP_BASE = 0.125
SOFTEN = 0.01
PART = 256
SLOTS = 24
CHIPS = 16
PLANE = 2 * CHIPS
COLUMN = 16
COLS = SLOTS * CHIPS
SHARE = SLOTS // 2
LANES = 128
LISTED = 32
RATES = 64
ALL_AXES = ("y", "h", "z", "l", "c")
PLANE_AXES = ("y", "h", "l", "c")
EXACT = lax.Precision.HIGHEST
F32 = jnp.float32
I32 = jnp.int32
BF16 = jnp.bfloat16
NT = (((1,), (1,)), ((), ()))
TN = (((0,), (0,)), ((), ()))


def predict(pos, vel, acc, jerk, elapsed):
    pred_pos = pos + elapsed * (vel + elapsed * (acc * 0.5 + elapsed * jerk / 6.0))
    pred_vel = vel + elapsed * (acc + elapsed * jerk * 0.5)
    return (pred_pos, pred_vel)


def correct(pos, vel, acc, jerk, new_acc, new_jerk, stride):
    half = 0.5 * stride
    square = stride * stride / 12.0
    vel_new = vel + half * (acc + new_acc) + square * (jerk - new_jerk)
    pos_new = pos + half * (vel + vel_new) + square * (acc - new_acc)
    return (pos_new, vel_new)


def iota(shape, axis):
    return lax.broadcasted_iota(I32, shape, axis)


def prepare_kernel(
    total, pos_h, vel_h, acc_h, jerk_h, weight_h, lev_h, active_h, counts_h, zsend, isend, place, slots, keep,
    jrows, srows, state, weight, levels, active, counts, sems,
):
    copies = [
        pltpu.make_async_copy(src, dst, sems.at[k])
        for k, (src, dst) in enumerate(
            (
                (pos_h, state.at[0]),
                (vel_h, state.at[1]),
                (acc_h, state.at[2]),
                (jerk_h, state.at[3]),
                (weight_h, weight),
                (lev_h, levels),
                (active_h, active),
                (counts_h, counts),
            )
        )
    ]
    for copy in copies:
        copy.start()
    for copy in copies:
        copy.wait()
    core = lax.axis_index("c")
    mass = weight[...] / total
    lev = levels[...]
    p, v, a, j = state[0], state[1], state[2], state[3]
    p1, v1 = predict(p, v, a, j, STEP_BASE)
    p2, v2 = predict(p, v, a, j, 2 * STEP_BASE)
    for k, part in enumerate((p, v, a, j)):
        keep[3 * k : 3 * k + 3] = part
    keep[12:13] = lev.astype(F32)
    keep[13:16] = jnp.zeros((3, PART), F32)
    jrows[0:3] = p1
    jrows[3:6] = v1
    jrows[6:7] = mass
    jrows[7:8] = jnp.zeros((1, PART), F32)
    jrows[8:11] = p2
    jrows[11:14] = v2
    jrows[14:15] = jnp.where(lev == 0, 0.0, mass)
    jrows[15:16] = jnp.zeros((1, PART), F32)
    rows = jrows[...]
    for k in range(COLUMN):
        zsend[k] = rows
    srows[...] = jnp.zeros(srows.shape, F32)
    srows[0:3] = p
    srows[3:6] = v
    srows[6:7] = mass
    srows[8:11] = p2
    srows[11:14] = v2
    srows[16:19] = a
    srows[19:22] = j

    n1, n2 = counts[0:1, 0:1], counts[0:1, 1:2]
    off0 = jnp.where(core == 1, SLOTS - n1, 0)
    off1 = jnp.where(core == 1, n1, 0)
    who = iota((PART, SLOTS), 0)
    slot = iota((PART, SLOTS), 1)
    a1 = ((who == active[0:1, :]) & (slot < n1)).astype(F32)
    a2 = ((who == active[1:2, :]) & (slot < n2)).astype(F32)
    col = iota((LANES, SLOTS), 0)
    cslot = iota((LANES, SLOTS), 1)
    first = (col == cslot + off0) & (cslot < n1)
    again = (col == cslot + off0 + RATES) & (cslot < n1)
    first_f = first.astype(F32)
    listed = jnp.dot(jnp.broadcast_to(lev.astype(F32), (8, PART)), a2, preferred_element_type=F32)
    live = iota((8, SLOTS), 1) < n2
    is0 = (live & (listed < 0.5)).astype(F32)
    is1 = (live & (listed > 0.5) & (listed < 1.5)).astype(F32)
    before = (iota((SLOTS, SLOTS), 0) < iota((SLOTS, SLOTS), 1)).astype(F32)
    rank0 = jnp.dot(is0, before, preferred_element_type=F32)[0:1].astype(I32)
    rank1 = jnp.dot(is1, before, preferred_element_type=F32)[0:1].astype(I32)
    second = ((col == rank1 + (off1 + LISTED)) & (is1[0:1] > 0.5)).astype(F32)
    held = ((col == rank0 + off0) & (is0[0:1] > 0.5)).astype(F32)
    spots = lax.dot_general(a1, first_f + again.astype(F32), NT, preferred_element_type=F32)
    spots = spots + lax.dot_general(a2, second, NT, preferred_element_type=F32)
    place[...] = spots
    slots[0] = first_f
    slots[1] = held + second
    picked = jnp.dot(srows[...], spots, precision=EXACT, preferred_element_type=F32)
    lane = iota((8, LANES), 1)
    payload = jnp.where(lane < LISTED, picked[0:8], jnp.where(lane < RATES, picked[8:16], picked[16:24]))
    for k in range(PLANE):
        isend[k] = payload


def rounded(value):
    return value.astype(BF16).astype(F32)


def split(value):
    high = rounded(value)
    middle = rounded(value - high)
    return high, middle, value - high - middle


def source_parts(rows, feats, values):
    count = rows.shape[0]
    row = iota(rows.shape, 0) % 8

    def ahead(value, by):
        return pltpu.roll(value, (count - by) % count, 0)

    square = rows * rows
    square = square + ahead(square, 1) + ahead(square, 2)
    cross = rows * ahead(rows, 3)
    cross = cross + ahead(cross, 1) + ahead(cross, 2)
    full = jnp.where(row == 6, 1.0, jnp.where(row == 7, ahead(square, count - 7), rows))
    high, middle, low = split(full)
    c_high, c_middle, c_low = split(cross)
    c_rows = jnp.where(row == 1, ahead(c_middle, count - 1), jnp.where(row == 2, ahead(c_low, count - 2), 0.0))
    c_rows = jnp.where(row == 0, c_high, c_rows)
    blank = jnp.zeros((8, PART), F32)
    for k in range(count // 8):
        here, cols = slice(8 * k, 8 * k + 8), slice(PART * k, PART * (k + 1))
        h, m, low_k = high[here], middle[here], low[here]
        feats[:, cols] = jnp.concatenate([h, h, m, m, h, low_k, c_rows[here], blank], axis=0).astype(BF16)
        weighed = rows[8 * k + 6 : 8 * k + 7] * jnp.where(row[here] == 6, 1.0, rows[here])
        weighed = jnp.where(row[here] == 7, 0.0, weighed)
        values[:, cols] = jnp.concatenate([*split(weighed), blank], axis=0).astype(BF16)


def target_parts(states):
    row = iota(states.shape, 0)
    square = states[0:3] * states[0:3]
    square = square[0:1] + square[1:2] + square[2:3] + SOFTEN
    cross = states[0:3] * states[3:6]
    cross = cross[0:1] + cross[1:2] + cross[2:3]
    turned = jnp.concatenate([states[3:6], states[0:3], states[6:8]], axis=0)
    near = jnp.where(row < 3, -2.0 * states, jnp.where(row < 6, 0.0, jnp.where(row == 6, square, 1.0)))
    rate = jnp.where(row < 6, -turned, jnp.where(row == 6, cross, 0.0))
    parts = []
    for full, one in ((near, 0.0), (rate, 1.0)):
        h, m, low = split(full)
        unit = jnp.where(row < 3, one, 0.0)
        parts.append(jnp.concatenate([h, m, h, m, low, h, unit, jnp.zeros_like(unit)], axis=0).astype(BF16))
    return parts


def pair_sums(states, feats, values, width):
    near, rate = target_parts(states)
    sum_w = sum_u = None
    for k in range(feats.shape[1] // width):
        cols = slice(width * k, width * (k + 1))
        feat, value = feats[:, cols], values[:, cols]
        dist = lax.dot_general(feat, near, TN, preferred_element_type=F32)
        radial = lax.dot_general(feat, rate, TN, preferred_element_type=F32)
        inv = lax.rsqrt(jnp.maximum(dist, SOFTEN))
        inv2 = inv * inv
        w = inv * inv2
        u = w * inv2 * radial
        total = []
        for term in (w, u):
            high = term.astype(BF16)
            low = (term - high.astype(F32)).astype(BF16)
            total.append(
                jnp.dot(value, high, preferred_element_type=F32) + jnp.dot(value, low, preferred_element_type=F32)
            )
        sum_w = total[0] if k == 0 else sum_w + total[0]
        sum_u = total[1] if k == 0 else sum_u + total[1]
    w = sum_w[0:8] + sum_w[8:16] + sum_w[16:24]
    u = sum_u[0:8] + sum_u[8:16] + sum_u[16:24]
    acc = w[0:3] - states[0:3] * w[6:7]
    jerk = w[3:6] - states[3:6] * w[6:7] - 3.0 * (u[0:3] - states[0:3] * u[6:7])
    return jnp.concatenate([acc, jerk, jnp.zeros((2, states.shape[1]), F32)], axis=0)


def first_kernel(zrecv, irecv, psend, known, other, feats, values):
    for q in range(CHIPS):
        block = irecv[2 * q] + irecv[2 * q + 1]
        here = slice(SLOTS * q, SLOTS * (q + 1))
        known[0:8, here] = block[:, 0:SLOTS]
        known[8:16, here] = block[:, RATES : RATES + SLOTS]
        other[:, here] = block[:, LISTED : LISTED + SLOTS]
    source_parts(zrecv[:, 0:8, :].reshape(8 * COLUMN, PART), feats, values)
    p1, v1 = predict(known[0:3], known[3:6], known[8:11], known[11:14], STEP_BASE)
    states = jnp.concatenate([p1, v1, jnp.zeros((2, COLS), F32)], axis=0)
    part = pair_sums(states, feats, values, 8 * PART)
    for k in range(PLANE):
        psend[k] = part


def later_kernel(zrecv, moved, other, out, feats, values):
    source_parts(zrecv[:, 8:16, :].reshape(8 * COLUMN, PART), feats, values)
    out[...] = pair_sums(jnp.concatenate([moved[...], other[...]], axis=1), feats, values, 4 * PART)


def update_kernel(precv, known, zsend, moved, mine):
    total = precv[0]
    for k in range(1, PLANE):
        total = total + precv[k]
    p, v, a, j = known[0:3], known[3:6], known[8:11], known[11:14]
    new_a, new_j = total[0:3], total[3:6]
    pos, vel = correct(p, v, a, j, new_a, new_j, STEP_BASE)
    p2, v2 = predict(pos, vel, new_a, new_j, STEP_BASE)
    moved[0:3] = p2
    moved[3:6] = v2
    moved[6:7] = known[6:7]
    moved[7:8] = jnp.zeros((1, COLS), F32)
    chip = (lax.axis_index("y") * 2 + lax.axis_index("h")) * 2 + lax.axis_index("l")
    core = lax.axis_index("c")
    spot = lax.rem(lax.axis_index("z"), 8) * 16
    row = iota((COLS, LANES), 0)
    lane = iota((COLS, LANES), 1)
    index = lane - spot
    share = ((row == index + (chip * SLOTS + core * SHARE)) & (index >= 0) & (index < SHARE)).astype(F32)
    block = ((row == lane + chip * SLOTS) & (lane < SLOTS)).astype(F32)
    payload = jnp.dot(moved[...], share, precision=EXACT, preferred_element_type=F32)
    for k in range(COLUMN):
        zsend[k] = payload
    mine[...] = jnp.dot(total, block, precision=EXACT, preferred_element_type=F32)


def last_kernel(zrecv, moved, other, part, fsend, feats, values, sums):
    halves = []
    for base in (0, 8):
        half = zrecv[base]
        for k in range(1, 8):
            half = half + zrecv[base + k]
        halves.append(half)
    source_parts(jnp.concatenate(halves, axis=1), feats, values)
    states = jnp.concatenate([moved[...], other[...]], axis=1)
    sums[...] = pair_sums(states, feats, values, PART) + part[...]
    for q in range(CHIPS):
        here = slice(SLOTS * q, SLOTS * (q + 1))
        there = slice(COLS + SLOTS * q, COLS + SLOTS * (q + 1))
        for k in (2 * q, 2 * q + 1):
            fsend[k] = jnp.zeros((8, LANES), F32)
            fsend[k, :, 0:SLOTS] = sums[:, here]
            fsend[k, :, LISTED : LISTED + SLOTS] = sums[:, there]


def finish_kernel(keep, frecv, mine, place, slots, pos_o, vel_o, acc_o, jerk_o, fresh):
    total = frecv[0]
    for k in range(1, PLANE):
        total = total + frecv[k]
    once = mine[...]
    fresh[:, 0, :] = jnp.dot(once, slots[0], precision=EXACT, preferred_element_type=F32)[0:6]
    fresh[:, 1, :] = jnp.dot(total, slots[1], precision=EXACT, preferred_element_type=F32)[0:6]
    lane = iota((8, LANES), 1)
    spots = place[...]
    spread = [
        lax.dot_general(jnp.where(lane < RATES, value, 0.0), spots, NT, precision=EXACT, preferred_element_type=F32)
        for value in (once, total)
    ]
    lev = keep[12:13].astype(I32)
    stride = STEP_BASE * jnp.left_shift(jnp.ones_like(lev), lev).astype(F32)
    p, v, a, j = keep[0:3], keep[3:6], keep[6:9], keep[9:12]
    for step in range(2):
        new_a, new_j = spread[step][0:3], spread[step][3:6]
        hit = lev <= step
        p_new, v_new = correct(p, v, a, j, new_a, new_j, stride)
        p, v = jnp.where(hit, p_new, p), jnp.where(hit, v_new, v)
        a, j = jnp.where(hit, new_a, a), jnp.where(hit, new_j, j)
    pos_o[...] = p
    vel_o[...] = v
    acc_o[...] = a
    jerk_o[...] = j


def call(kernel, ins, outs, scratch=(), far=0, mib=8):
    vmem = pl.BlockSpec(memory_space=pltpu.VMEM)
    return pl.pallas_call(
        kernel,
        out_shape=[jax.ShapeDtypeStruct(s, F32) for s in outs],
        in_specs=[pl.BlockSpec(memory_space=pltpu.HBM)] * far + [vmem] * (len(ins) - far),
        out_specs=[vmem] * len(outs),
        scratch_shapes=list(scratch),
        compiler_params=pltpu.CompilerParams(vmem_limit_bytes=mib * 1024 * 1024),
    )(*ins)


def operands(sources):
    return [pltpu.VMEM((64, sources), BF16), pltpu.VMEM((32, sources), BF16)]


def exchange(value, axes):
    return lax.all_to_all(value, axes, 0, 0, tiled=True)


def body(positions, velocities, accelerations, jerks, mass_weight, levels, active, counts):
    total_part = PART * lax.axis_size(ALL_AXES)
    lev = levels.reshape(1, PART)
    state = (positions, velocities, accelerations, jerks)

    def prepare(*refs):
        prepare_kernel(total_part, *refs)

    zsend, isend, place, slots, keep = call(
        prepare,
        (*state, mass_weight.reshape(1, PART), lev, active, counts.reshape(1, 2)),
        [(COLUMN, 16, PART), (PLANE, 8, LANES), (PART, LANES), (2, LANES, SLOTS), (16, PART)],
        [
            pltpu.VMEM((16, PART), F32),
            pltpu.VMEM((24, PART), F32),
            pltpu.VMEM((4, 3, PART), F32),
            pltpu.VMEM((1, PART), F32),
            pltpu.VMEM((1, PART), I32),
            pltpu.VMEM((2, SLOTS), I32),
            pltpu.VMEM((1, 2), I32),
            pltpu.SemaphoreType.DMA((8,)),
        ],
        far=8,
        mib=60,
    )
    irecv = exchange(isend, PLANE_AXES)
    zrecv = exchange(zsend, "z")
    psend, known, other = call(
        first_kernel, (zrecv, irecv), [(PLANE, 8, COLS), (16, COLS), (8, COLS)], operands(COLUMN * PART), mib=24
    )
    precv = exchange(psend, PLANE_AXES)
    zsend2, moved, mine = call(update_kernel, (precv, known), [(COLUMN, 8, LANES), (8, COLS), (8, LANES)])
    zrecv2 = exchange(zsend2, "z")
    (part,) = call(later_kernel, (zrecv, moved, other), [(8, 2 * COLS)], operands(COLUMN * PART), mib=24)
    (fsend,) = call(
        last_kernel,
        (zrecv2, moved, other, part),
        [(PLANE, 8, LANES)],
        operands(PART) + [pltpu.VMEM((8, 2 * COLS), F32)],
    )
    frecv = exchange(fsend, PLANE_AXES)
    *state, fresh = call(
        finish_kernel,
        (keep, frecv, mine, place, slots),
        [(3, PART)] * 4 + [(6, 2, SLOTS)],
    )
    return (*state, fresh.transpose(1, 0, 2))


def solution(mesh):
    fine = Mesh(mesh.devices.reshape(4, 2, 16, 2, 2), ALL_AXES)
    rows, flat = P(None, ALL_AXES), P(ALL_AXES)
    in_specs = (rows, rows, rows, rows, flat, flat, rows, rows)
    out_specs = (rows, rows, rows, rows, P(None, None, ALL_AXES))
    return jax.shard_map(body, mesh=fine, in_specs=in_specs, out_specs=out_specs, check_vma=False)
```

```python
import jax
import jax.numpy as jnp
from jax import lax
from jax.experimental import pallas as pl
from jax.experimental.pallas import tpu as pltpu
from jax.sharding import Mesh, PartitionSpec as P

STEP_BASE = 0.125
SOFTEN = 0.01
PART = 256
SLOTS = 24
CHIPS = 16
PLANE = 2 * CHIPS
COLUMN = 16
COLS = SLOTS * CHIPS
SHARE = SLOTS // 2
LANES = 128
LISTED = 32
RATES = 64
ALL_AXES = ("a", "b", "h", "z", "l", "c")
PLANE_AXES = ("a", "b", "h", "l", "c")
STAGES = (("l", "c"), "h", "b", "a")
EXACT = lax.Precision.HIGHEST
F32 = jnp.float32
I32 = jnp.int32
BF16 = jnp.bfloat16
NT = (((1,), (1,)), ((), ()))
TN = (((0,), (0,)), ((), ()))


def predict(pos, vel, acc, jerk, elapsed):
    pred_pos = pos + elapsed * (vel + elapsed * (acc * 0.5 + elapsed * jerk / 6.0))
    pred_vel = vel + elapsed * (acc + elapsed * jerk * 0.5)
    return (pred_pos, pred_vel)


def correct(pos, vel, acc, jerk, new_acc, new_jerk, stride):
    half = 0.5 * stride
    square = stride * stride / 12.0
    vel_new = vel + half * (acc + new_acc) + square * (jerk - new_jerk)
    pos_new = pos + half * (vel + vel_new) + square * (acc - new_acc)
    return (pos_new, vel_new)


def iota(shape, axis):
    return lax.broadcasted_iota(I32, shape, axis)


def prepare_kernel(
    total, pos_h, vel_h, acc_h, jerk_h, weight_h, lev_h, active_h, counts_h, zsend, isend, place, slots, keep,
    jrows, srows, state, weight, levels, active, counts, sems,
):
    copies = [
        pltpu.make_async_copy(src, dst, sems.at[k])
        for k, (src, dst) in enumerate(
            (
                (pos_h, state.at[0]),
                (vel_h, state.at[1]),
                (acc_h, state.at[2]),
                (jerk_h, state.at[3]),
                (weight_h, weight),
                (lev_h, levels),
                (active_h, active),
                (counts_h, counts),
            )
        )
    ]
    for copy in copies:
        copy.start()
    for copy in copies:
        copy.wait()
    core = lax.axis_index("c")
    mass = weight[...] / total
    lev = levels[...]
    p, v, a, j = state[0], state[1], state[2], state[3]
    p1, v1 = predict(p, v, a, j, STEP_BASE)
    p2, v2 = predict(p, v, a, j, 2 * STEP_BASE)
    for k, part in enumerate((p, v, a, j)):
        keep[3 * k : 3 * k + 3] = part
    keep[12:13] = lev.astype(F32)
    keep[13:16] = jnp.zeros((3, PART), F32)
    jrows[0:3] = p1
    jrows[3:6] = v1
    jrows[6:7] = mass
    jrows[7:8] = jnp.zeros((1, PART), F32)
    jrows[8:11] = p2
    jrows[11:14] = v2
    jrows[14:15] = jnp.where(lev == 0, 0.0, mass)
    jrows[15:16] = jnp.zeros((1, PART), F32)
    rows = jrows[...]
    for k in range(COLUMN):
        zsend[k] = rows
    srows[...] = jnp.zeros(srows.shape, F32)
    srows[0:3] = p
    srows[3:6] = v
    srows[6:7] = mass
    srows[8:11] = p2
    srows[11:14] = v2
    srows[16:19] = a
    srows[19:22] = j

    n1, n2 = counts[0:1, 0:1], counts[0:1, 1:2]
    off0 = jnp.where(core == 1, SLOTS - n1, 0)
    off1 = jnp.where(core == 1, n1, 0)
    who = iota((PART, SLOTS), 0)
    slot = iota((PART, SLOTS), 1)
    a1 = ((who == active[0:1, :]) & (slot < n1)).astype(F32)
    a2 = ((who == active[1:2, :]) & (slot < n2)).astype(F32)
    col = iota((LANES, SLOTS), 0)
    cslot = iota((LANES, SLOTS), 1)
    first = (col == cslot + off0) & (cslot < n1)
    again = (col == cslot + off0 + RATES) & (cslot < n1)
    first_f = first.astype(F32)
    listed = jnp.dot(jnp.broadcast_to(lev.astype(F32), (8, PART)), a2, preferred_element_type=F32)
    live = iota((8, SLOTS), 1) < n2
    is0 = (live & (listed < 0.5)).astype(F32)
    is1 = (live & (listed > 0.5) & (listed < 1.5)).astype(F32)
    before = (iota((SLOTS, SLOTS), 0) < iota((SLOTS, SLOTS), 1)).astype(F32)
    rank0 = jnp.dot(is0, before, preferred_element_type=F32)[0:1].astype(I32)
    rank1 = jnp.dot(is1, before, preferred_element_type=F32)[0:1].astype(I32)
    second = ((col == rank1 + (off1 + LISTED)) & (is1[0:1] > 0.5)).astype(F32)
    held = ((col == rank0 + off0) & (is0[0:1] > 0.5)).astype(F32)
    spots = lax.dot_general(a1, first_f + again.astype(F32), NT, preferred_element_type=F32)
    spots = spots + lax.dot_general(a2, second, NT, preferred_element_type=F32)
    place[...] = spots
    slots[0] = first_f
    slots[1] = held + second
    picked = jnp.dot(srows[...], spots, precision=EXACT, preferred_element_type=F32)
    lane = iota((8, LANES), 1)
    payload = jnp.where(lane < LISTED, picked[0:8], jnp.where(lane < RATES, picked[8:16], picked[16:24]))
    isend[...] = payload


def rounded(value):
    return value.astype(BF16).astype(F32)


def split(value):
    high = rounded(value)
    middle = rounded(value - high)
    return high, middle, value - high - middle


def source_parts(rows, feats, values):
    count = rows.shape[0]
    row = iota(rows.shape, 0) % 8

    def ahead(value, by):
        return pltpu.roll(value, (count - by) % count, 0)

    square = rows * rows
    square = square + ahead(square, 1) + ahead(square, 2)
    cross = rows * ahead(rows, 3)
    cross = cross + ahead(cross, 1) + ahead(cross, 2)
    full = jnp.where(row == 6, 1.0, jnp.where(row == 7, ahead(square, count - 7), rows))
    high, middle, low = split(full)
    c_high, c_middle, c_low = split(cross)
    c_rows = jnp.where(row == 1, ahead(c_middle, count - 1), jnp.where(row == 2, ahead(c_low, count - 2), 0.0))
    c_rows = jnp.where(row == 0, c_high, c_rows)
    blank = jnp.zeros((8, PART), F32)
    for k in range(count // 8):
        here, cols = slice(8 * k, 8 * k + 8), slice(PART * k, PART * (k + 1))
        h, m, low_k = high[here], middle[here], low[here]
        feats[:, cols] = jnp.concatenate([h, h, m, m, h, low_k, c_rows[here], blank], axis=0).astype(BF16)
        weighed = rows[8 * k + 6 : 8 * k + 7] * jnp.where(row[here] == 6, 1.0, rows[here])
        weighed = jnp.where(row[here] == 7, 0.0, weighed)
        values[:, cols] = jnp.concatenate([*split(weighed), blank], axis=0).astype(BF16)


def target_parts(states):
    row = iota(states.shape, 0)
    square = states[0:3] * states[0:3]
    square = square[0:1] + square[1:2] + square[2:3] + SOFTEN
    cross = states[0:3] * states[3:6]
    cross = cross[0:1] + cross[1:2] + cross[2:3]
    turned = jnp.concatenate([states[3:6], states[0:3], states[6:8]], axis=0)
    near = jnp.where(row < 3, -2.0 * states, jnp.where(row < 6, 0.0, jnp.where(row == 6, square, 1.0)))
    rate = jnp.where(row < 6, -turned, jnp.where(row == 6, cross, 0.0))
    parts = []
    for full, one in ((near, 0.0), (rate, 1.0)):
        h, m, low = split(full)
        unit = jnp.where(row < 3, one, 0.0)
        parts.append(jnp.concatenate([h, m, h, m, low, h, unit, jnp.zeros_like(unit)], axis=0).astype(BF16))
    return parts


def pair_sums(states, feats, values, width):
    count = states.shape[1]
    both = jnp.concatenate(target_parts(states), axis=1)
    total = None
    for k in range(feats.shape[1] // width):
        cols = slice(width * k, width * (k + 1))
        product = lax.dot_general(feats[:, cols], both, TN, preferred_element_type=F32)
        inv = lax.rsqrt(jnp.maximum(product[:, :count], SOFTEN))
        inv2 = inv * inv
        w = inv * inv2
        terms = (w, w * inv2 * product[:, count:])
        high = [term.astype(BF16) for term in terms]
        low = [(term - part.astype(F32)).astype(BF16) for term, part in zip(terms, high)]
        for part in (high, low):
            term = jnp.dot(values[:, cols], jnp.concatenate(part, axis=1), preferred_element_type=F32)
            total = term if total is None else total + term
    sum_w, sum_u = total[:, :count], total[:, count:]
    w = sum_w[0:8] + sum_w[8:16] + sum_w[16:24]
    u = sum_u[0:8] + sum_u[8:16] + sum_u[16:24]
    acc = w[0:3] - states[0:3] * w[6:7]
    jerk = w[3:6] - states[3:6] * w[6:7] - 3.0 * (u[0:3] - states[0:3] * u[6:7])
    return jnp.concatenate([acc, jerk, jnp.zeros((2, states.shape[1]), F32)], axis=0)


def first_kernel(zrecv, irecv, psend, known, other, feats, values):
    for q in range(CHIPS):
        block = irecv[2 * q] + irecv[2 * q + 1]
        here = slice(SLOTS * q, SLOTS * (q + 1))
        known[0:8, here] = block[:, 0:SLOTS]
        known[8:16, here] = block[:, RATES : RATES + SLOTS]
        other[:, here] = block[:, LISTED : LISTED + SLOTS]
    source_parts(zrecv[:, 0:8, :].reshape(8 * COLUMN, PART), feats, values)
    p1, v1 = predict(known[0:3], known[3:6], known[8:11], known[11:14], STEP_BASE)
    states = jnp.concatenate([p1, v1, jnp.zeros((2, COLS), F32)], axis=0)
    part = pair_sums(states, feats, values, 8 * PART)
    halves = [jnp.concatenate([part[3 * row + k : 3 * row + k + 1] for k in range(3)], axis=1) for row in range(2)]
    both = jnp.concatenate(halves, axis=0)
    for k in range(PLANE):
        psend[k] = both


def later_kernel(zrecv, moved, other, out, feats, values):
    source_parts(zrecv[:, 8:16, :].reshape(8 * COLUMN, PART), feats, values)
    out[:, 0:COLS] = pair_sums(moved[...], feats, values, 8 * PART)
    out[:, COLS:] = pair_sums(other[...], feats, values, 8 * PART)


def update_kernel(precv, known, zsend, moved, mine):
    both = precv[0]
    for k in range(1, PLANE):
        both = both + precv[k]
    total = [both[row : row + 1, COLS * k : COLS * (k + 1)] for row in range(2) for k in range(3)]
    total = jnp.concatenate([*total, jnp.zeros((2, COLS), F32)], axis=0)
    p, v, a, j = known[0:3], known[3:6], known[8:11], known[11:14]
    new_a, new_j = total[0:3], total[3:6]
    pos, vel = correct(p, v, a, j, new_a, new_j, STEP_BASE)
    p2, v2 = predict(pos, vel, new_a, new_j, STEP_BASE)
    moved[0:3] = p2
    moved[3:6] = v2
    moved[6:7] = known[6:7]
    moved[7:8] = jnp.zeros((1, COLS), F32)
    chip = lax.axis_index("a")
    for axis in ("b", "h", "l"):
        chip = chip * 2 + lax.axis_index(axis)
    core = lax.axis_index("c")
    row = iota((COLS, LANES), 0)
    lane = iota((COLS, LANES), 1)
    index = lane % 16
    share = ((row == index + (chip * SLOTS + core * SHARE)) & (index < SHARE)).astype(F32)
    block = ((row == lane + chip * SLOTS) & (lane < SLOTS)).astype(F32)
    payload = jnp.dot(moved[...], share, precision=EXACT, preferred_element_type=F32)
    payload = jnp.where(iota((8, LANES), 0) == iota((8, LANES), 1) // 16, payload, 0.0)
    payload = jnp.sum(payload, axis=0, keepdims=True)
    for k in range(COLUMN):
        zsend[k] = payload
    mine[...] = jnp.dot(total, block, precision=EXACT, preferred_element_type=F32)


def last_kernel(zrecv, moved, other, part, fsend, feats, values, rows, sums):
    lane = iota((8, LANES), 1)
    rows[...] = jnp.zeros(rows.shape, F32)
    for half in range(2):
        packed = zrecv[8 * half : 8 * half + 8, 0, :]
        for k in range(7):
            item = jnp.where(lane < 16, pltpu.roll(packed, (LANES - 16 * k) % LANES, 1), 0.0)
            item = pltpu.roll(item, 0, 1, stride=16, stride_axis=0)
            rows[k : k + 1, LANES * half : LANES * (half + 1)] = jnp.sum(item, axis=0, keepdims=True)
    source_parts(rows[...], feats, values)
    states = jnp.concatenate([moved[...], other[...]], axis=1)
    sums[...] = pair_sums(states, feats, values, PART) + part[...]
    for q in range(CHIPS):
        here = slice(SLOTS * q, SLOTS * (q + 1))
        there = slice(COLS + SLOTS * q, COLS + SLOTS * (q + 1))
        for k in (2 * q, 2 * q + 1):
            fsend[k] = jnp.zeros((8, LANES), F32)
            fsend[k, :, 0:SLOTS] = sums[:, here]
            fsend[k, :, LISTED : LISTED + SLOTS] = sums[:, there]


def finish_kernel(keep, frecv, mine, place, slots, pos_o, vel_o, acc_o, jerk_o, fresh):
    total = frecv[0]
    for k in range(1, PLANE):
        total = total + frecv[k]
    once = mine[...]
    fresh[:, 0, :] = jnp.dot(once, slots[0], precision=EXACT, preferred_element_type=F32)[0:6]
    fresh[:, 1, :] = jnp.dot(total, slots[1], precision=EXACT, preferred_element_type=F32)[0:6]
    lane = iota((8, LANES), 1)
    spots = place[...]
    spread = [
        lax.dot_general(jnp.where(lane < RATES, value, 0.0), spots, NT, precision=EXACT, preferred_element_type=F32)
        for value in (once, total)
    ]
    lev = keep[12:13].astype(I32)
    stride = STEP_BASE * jnp.left_shift(jnp.ones_like(lev), lev).astype(F32)
    p, v, a, j = keep[0:3], keep[3:6], keep[6:9], keep[9:12]
    for step in range(2):
        new_a, new_j = spread[step][0:3], spread[step][3:6]
        hit = lev <= step
        p_new, v_new = correct(p, v, a, j, new_a, new_j, stride)
        p, v = jnp.where(hit, p_new, p), jnp.where(hit, v_new, v)
        a, j = jnp.where(hit, new_a, a), jnp.where(hit, new_j, j)
    pos_o[...] = p
    vel_o[...] = v
    acc_o[...] = a
    jerk_o[...] = j


def call(kernel, ins, outs, scratch=(), far=0, mib=8):
    vmem = pl.BlockSpec(memory_space=pltpu.VMEM)
    return pl.pallas_call(
        kernel,
        out_shape=[jax.ShapeDtypeStruct(s, F32) for s in outs],
        in_specs=[pl.BlockSpec(memory_space=pltpu.HBM)] * far + [vmem] * (len(ins) - far),
        out_specs=[vmem] * len(outs),
        scratch_shapes=list(scratch),
        compiler_params=pltpu.CompilerParams(vmem_limit_bytes=mib * 1024 * 1024),
    )(*ins)


def operands(sources):
    return [pltpu.VMEM((64, sources), BF16), pltpu.VMEM((32, sources), BF16)]


def gathered(value):
    for axes in STAGES:
        value = lax.all_gather(value, axes, tiled=True)
    return value.reshape(PLANE, 8, LANES)


def exchange(value, axes):
    return lax.all_to_all(value, axes, 0, 0, tiled=True)


def body(positions, velocities, accelerations, jerks, mass_weight, levels, active, counts):
    total_part = PART * lax.axis_size(ALL_AXES)
    lev = levels.reshape(1, PART)
    state = (positions, velocities, accelerations, jerks)

    def prepare(*refs):
        prepare_kernel(total_part, *refs)

    zsend, isend, place, slots, keep = call(
        prepare,
        (*state, mass_weight.reshape(1, PART), lev, active, counts.reshape(1, 2)),
        [(COLUMN, 16, PART), (8, LANES), (PART, LANES), (2, LANES, SLOTS), (16, PART)],
        [
            pltpu.VMEM((16, PART), F32),
            pltpu.VMEM((24, PART), F32),
            pltpu.VMEM((4, 3, PART), F32),
            pltpu.VMEM((1, PART), F32),
            pltpu.VMEM((1, PART), I32),
            pltpu.VMEM((2, SLOTS), I32),
            pltpu.VMEM((1, 2), I32),
            pltpu.SemaphoreType.DMA((8,)),
        ],
        far=8,
        mib=60,
    )
    irecv = gathered(isend)
    zrecv = exchange(zsend, "z")
    psend, known, other = call(
        first_kernel, (zrecv, irecv), [(PLANE, 2, 3 * COLS), (16, COLS), (8, COLS)], operands(COLUMN * PART), mib=24
    )
    precv = exchange(psend, PLANE_AXES)
    zsend2, moved, mine = call(update_kernel, (precv, known), [(COLUMN, 1, LANES), (8, COLS), (8, LANES)])
    zrecv2 = exchange(zsend2, "z")
    (part,) = call(later_kernel, (zrecv, moved, other), [(8, 2 * COLS)], operands(COLUMN * PART), mib=24)
    (fsend,) = call(
        last_kernel,
        (zrecv2, moved, other, part),
        [(PLANE, 8, LANES)],
        operands(PART) + [pltpu.VMEM((8, PART), F32), pltpu.VMEM((8, 2 * COLS), F32)],
    )
    frecv = exchange(fsend, PLANE_AXES)
    *state, fresh = call(
        finish_kernel,
        (keep, frecv, mine, place, slots),
        [(3, PART)] * 4 + [(6, 2, SLOTS)],
    )
    return (*state, fresh.transpose(1, 0, 2))


def solution(mesh):
    fine = Mesh(mesh.devices.reshape(2, 2, 2, 16, 2, 2), ALL_AXES)
    rows, flat = P(None, ALL_AXES), P(ALL_AXES)
    in_specs = (rows, rows, rows, rows, flat, flat, rows, rows)
    out_specs = (rows, rows, rows, rows, P(None, None, ALL_AXES))
    return jax.shard_map(body, mesh=fine, in_specs=in_specs, out_specs=out_specs, check_vma=False)
```

```python
import jax
import jax.numpy as jnp
from jax import lax
from jax.experimental import pallas as pl
from jax.experimental.pallas import tpu as pltpu
from jax.sharding import Mesh, PartitionSpec as P

STEP_BASE = 0.125
SOFTEN = 0.01
PART = 256
SLOTS = 24
CHIPS = 16
PLANE = 2 * CHIPS
COLUMN = 16
COLS = SLOTS * CHIPS
SHARE = SLOTS // 2
LANES = 128
LISTED = 32
RATES = 64
ALL_AXES = ("a", "b", "h", "z", "l", "c")
PLANE_AXES = ("a", "b", "h", "l", "c")
STAGES = (("l", "c"), "h", "b", "a")
EXACT = lax.Precision.HIGHEST
F32 = jnp.float32
I32 = jnp.int32
BF16 = jnp.bfloat16
NT = (((1,), (1,)), ((), ()))
TN = (((0,), (0,)), ((), ()))


def predict(pos, vel, acc, jerk, elapsed):
    pred_pos = pos + elapsed * (vel + elapsed * (acc * 0.5 + elapsed * jerk / 6.0))
    pred_vel = vel + elapsed * (acc + elapsed * jerk * 0.5)
    return (pred_pos, pred_vel)


def correct(pos, vel, acc, jerk, new_acc, new_jerk, stride):
    half = 0.5 * stride
    square = stride * stride / 12.0
    vel_new = vel + half * (acc + new_acc) + square * (jerk - new_jerk)
    pos_new = pos + half * (vel + vel_new) + square * (acc - new_acc)
    return (pos_new, vel_new)


def iota(shape, axis):
    return lax.broadcasted_iota(I32, shape, axis)


def prepare_kernel(
    total, pos_h, vel_h, acc_h, jerk_h, weight_h, lev_h, active_h, counts_h, zsend, isend, place, slots, keep,
    jrows, srows, state, weight, levels, active, counts, sems,
):
    copies = [
        pltpu.make_async_copy(src, dst, sems.at[k])
        for k, (src, dst) in enumerate(
            (
                (pos_h, state.at[0]),
                (vel_h, state.at[1]),
                (acc_h, state.at[2]),
                (jerk_h, state.at[3]),
                (weight_h, weight),
                (lev_h, levels),
                (active_h, active),
                (counts_h, counts),
            )
        )
    ]
    for copy in copies:
        copy.start()
    for copy in copies:
        copy.wait()
    core = lax.axis_index("c")
    mass = weight[...] / total
    lev = levels[...]
    p, v, a, j = state[0], state[1], state[2], state[3]
    p1, v1 = predict(p, v, a, j, STEP_BASE)
    p2, v2 = predict(p, v, a, j, 2 * STEP_BASE)
    for k, part in enumerate((p, v, a, j)):
        keep[3 * k : 3 * k + 3] = part
    keep[12:13] = lev.astype(F32)
    keep[13:16] = jnp.zeros((3, PART), F32)
    jrows[0:3] = p1
    jrows[3:6] = v1
    jrows[6:7] = mass
    jrows[7:8] = jnp.zeros((1, PART), F32)
    jrows[8:11] = p2
    jrows[11:14] = v2
    jrows[14:15] = jnp.where(lev == 0, 0.0, mass)
    jrows[15:16] = jnp.zeros((1, PART), F32)
    rows = jrows[...]
    for k in range(COLUMN):
        zsend[k] = rows
    srows[...] = jnp.zeros(srows.shape, F32)
    srows[0:3] = p
    srows[3:6] = v
    srows[6:7] = mass
    srows[8:11] = p2
    srows[11:14] = v2
    srows[16:19] = a
    srows[19:22] = j

    n1, n2 = counts[0:1, 0:1], counts[0:1, 1:2]
    off0 = jnp.where(core == 1, SLOTS - n1, 0)
    off1 = jnp.where(core == 1, n1, 0)
    who = iota((PART, SLOTS), 0)
    slot = iota((PART, SLOTS), 1)
    a1 = ((who == active[0:1, :]) & (slot < n1)).astype(F32)
    a2 = ((who == active[1:2, :]) & (slot < n2)).astype(F32)
    col = iota((LANES, SLOTS), 0)
    cslot = iota((LANES, SLOTS), 1)
    first = (col == cslot + off0) & (cslot < n1)
    again = (col == cslot + off0 + RATES) & (cslot < n1)
    first_f = first.astype(F32)
    listed = jnp.dot(jnp.broadcast_to(lev.astype(F32), (8, PART)), a2, preferred_element_type=F32)
    live = iota((8, SLOTS), 1) < n2
    is0 = (live & (listed < 0.5)).astype(F32)
    is1 = (live & (listed > 0.5) & (listed < 1.5)).astype(F32)
    before = (iota((SLOTS, SLOTS), 0) < iota((SLOTS, SLOTS), 1)).astype(F32)
    rank0 = jnp.dot(is0, before, preferred_element_type=F32)[0:1].astype(I32)
    rank1 = jnp.dot(is1, before, preferred_element_type=F32)[0:1].astype(I32)
    second = ((col == rank1 + (off1 + LISTED)) & (is1[0:1] > 0.5)).astype(F32)
    held = ((col == rank0 + off0) & (is0[0:1] > 0.5)).astype(F32)
    spots = lax.dot_general(a1, first_f + again.astype(F32), NT, preferred_element_type=F32)
    spots = spots + lax.dot_general(a2, second, NT, preferred_element_type=F32)
    place[...] = spots
    slots[0] = first_f
    slots[1] = held + second
    picked = jnp.dot(srows[...], spots, precision=EXACT, preferred_element_type=F32)
    lane = iota((8, LANES), 1)
    payload = jnp.where(lane < LISTED, picked[0:8], jnp.where(lane < RATES, picked[8:16], picked[16:24]))
    isend[...] = payload


def rounded(value):
    return value.astype(BF16).astype(F32)


def split(value):
    high = rounded(value)
    middle = rounded(value - high)
    return high, middle, value - high - middle


def middle_of(states):
    mean = jnp.sum(states, axis=1, keepdims=True) / states.shape[1]
    return jnp.where(iota(mean.shape, 0) < 6, mean, 0.0)


def source_parts(rows, middle, feats, values):
    count = rows.shape[0]
    rows = rows - jnp.concatenate([middle] * (count // 8), axis=0)
    row = iota(rows.shape, 0) % 8

    def ahead(value, by):
        return pltpu.roll(value, (count - by) % count, 0)

    square = rows * rows
    square = square + ahead(square, 1) + ahead(square, 2)
    cross = rows * ahead(rows, 3)
    cross = cross + ahead(cross, 1) + ahead(cross, 2)
    full = jnp.where(row == 6, 1.0, jnp.where(row == 7, ahead(square, count - 7), rows))
    high, middle, low = split(full)
    c_high, c_middle, c_low = split(cross)
    c_rows = jnp.where(row == 1, ahead(c_middle, count - 1), jnp.where(row == 2, ahead(c_low, count - 2), 0.0))
    c_rows = jnp.where(row == 0, c_high, c_rows)
    blank = jnp.zeros((8, PART), F32)
    for k in range(count // 8):
        here, cols = slice(8 * k, 8 * k + 8), slice(PART * k, PART * (k + 1))
        h, m, low_k = high[here], middle[here], low[here]
        feats[:, cols] = jnp.concatenate([h, h, m, m, h, low_k, c_rows[here], blank], axis=0).astype(BF16)
        weighed = rows[8 * k + 6 : 8 * k + 7] * jnp.where(row[here] == 6, 1.0, rows[here])
        weighed = jnp.where(row[here] == 7, 0.0, weighed)
        values[:, cols] = jnp.concatenate([*split(weighed), blank], axis=0).astype(BF16)


def target_parts(states):
    row = iota(states.shape, 0)
    square = states[0:3] * states[0:3]
    square = square[0:1] + square[1:2] + square[2:3] + SOFTEN
    cross = states[0:3] * states[3:6]
    cross = cross[0:1] + cross[1:2] + cross[2:3]
    turned = jnp.concatenate([states[3:6], states[0:3], states[6:8]], axis=0)
    near = jnp.where(row < 3, -2.0 * states, jnp.where(row < 6, 0.0, jnp.where(row == 6, square, 1.0)))
    rate = jnp.where(row < 6, -turned, jnp.where(row == 6, cross, 0.0))
    parts = []
    for full, one in ((near, 0.0), (rate, 1.0)):
        h, m, low = split(full)
        unit = jnp.where(row < 3, one, 0.0)
        parts.append(jnp.concatenate([h, m, h, m, low, h, unit, jnp.zeros_like(unit)], axis=0).astype(BF16))
    return parts


def pair_sums(states, feats, values, width):
    count = states.shape[1]
    both = jnp.concatenate(target_parts(states), axis=1)
    total = None
    for k in range(feats.shape[1] // width):
        cols = slice(width * k, width * (k + 1))
        product = lax.dot_general(feats[:, cols], both, TN, preferred_element_type=F32)
        inv = lax.rsqrt(jnp.maximum(product[:, :count], SOFTEN))
        inv2 = inv * inv
        w = inv * inv2
        terms = (w, w * inv2 * product[:, count:])
        high = [term.astype(BF16) for term in terms]
        low = [(term - part.astype(F32)).astype(BF16) for term, part in zip(terms, high)]
        for part in (high, low):
            term = jnp.dot(values[:, cols], jnp.concatenate(part, axis=1), preferred_element_type=F32)
            total = term if total is None else total + term
    sum_w, sum_u = total[:, :count], total[:, count:]
    w = sum_w[0:8] + sum_w[8:16] + sum_w[16:24]
    u = sum_u[0:8] + sum_u[8:16] + sum_u[16:24]
    acc = w[0:3] - states[0:3] * w[6:7]
    jerk = w[3:6] - states[3:6] * w[6:7] - 3.0 * (u[0:3] - states[0:3] * u[6:7])
    return jnp.concatenate([acc, jerk, jnp.zeros((2, states.shape[1]), F32)], axis=0)


def first_kernel(zrecv, irecv, psend, known, other, feats, values):
    for q in range(CHIPS):
        block = irecv[2 * q] + irecv[2 * q + 1]
        here = slice(SLOTS * q, SLOTS * (q + 1))
        known[0:8, here] = block[:, 0:SLOTS]
        known[8:16, here] = block[:, RATES : RATES + SLOTS]
        other[:, here] = block[:, LISTED : LISTED + SLOTS]
    p1, v1 = predict(known[0:3], known[3:6], known[8:11], known[11:14], STEP_BASE)
    states = jnp.concatenate([p1, v1, jnp.zeros((2, COLS), F32)], axis=0)
    middle = middle_of(states)
    source_parts(zrecv[:, 0:8, :].reshape(8 * COLUMN, PART), middle, feats, values)
    part = pair_sums(states - middle, feats, values, 8 * PART)
    halves = [jnp.concatenate([part[3 * row + k : 3 * row + k + 1] for k in range(3)], axis=1) for row in range(2)]
    both = jnp.concatenate(halves, axis=0)
    for k in range(PLANE):
        psend[k] = both


def later_kernel(zrecv, moved, other, out, feats, values):
    middle = middle_of(moved[...])
    source_parts(zrecv[:, 8:16, :].reshape(8 * COLUMN, PART), middle, feats, values)
    out[:, 0:COLS] = pair_sums(moved[...] - middle, feats, values, 8 * PART)
    out[:, COLS:] = pair_sums(other[...] - middle, feats, values, 8 * PART)


def update_kernel(precv, known, zsend, moved, mine):
    both = precv[0]
    for k in range(1, PLANE):
        both = both + precv[k]
    total = [both[row : row + 1, COLS * k : COLS * (k + 1)] for row in range(2) for k in range(3)]
    total = jnp.concatenate([*total, jnp.zeros((2, COLS), F32)], axis=0)
    p, v, a, j = known[0:3], known[3:6], known[8:11], known[11:14]
    new_a, new_j = total[0:3], total[3:6]
    pos, vel = correct(p, v, a, j, new_a, new_j, STEP_BASE)
    p2, v2 = predict(pos, vel, new_a, new_j, STEP_BASE)
    moved[0:3] = p2
    moved[3:6] = v2
    moved[6:7] = known[6:7]
    moved[7:8] = jnp.zeros((1, COLS), F32)
    chip = lax.axis_index("a")
    for axis in ("b", "h", "l"):
        chip = chip * 2 + lax.axis_index(axis)
    core = lax.axis_index("c")
    row = iota((COLS, LANES), 0)
    lane = iota((COLS, LANES), 1)
    index = lane % 16
    share = ((row == index + (chip * SLOTS + core * SHARE)) & (index < SHARE)).astype(F32)
    block = ((row == lane + chip * SLOTS) & (lane < SLOTS)).astype(F32)
    payload = jnp.dot(moved[...], share, precision=EXACT, preferred_element_type=F32)
    payload = jnp.where(iota((8, LANES), 0) == iota((8, LANES), 1) // 16, payload, 0.0)
    payload = jnp.sum(payload, axis=0, keepdims=True)
    for k in range(COLUMN):
        zsend[k] = payload
    mine[...] = jnp.dot(total, block, precision=EXACT, preferred_element_type=F32)


def last_kernel(zrecv, moved, other, part, fsend, feats, values, rows, sums):
    lane = iota((8, LANES), 1)
    rows[...] = jnp.zeros(rows.shape, F32)
    for half in range(2):
        packed = zrecv[8 * half : 8 * half + 8, 0, :]
        for k in range(7):
            item = jnp.where(lane < 16, pltpu.roll(packed, (LANES - 16 * k) % LANES, 1), 0.0)
            item = pltpu.roll(item, 0, 1, stride=16, stride_axis=0)
            rows[k : k + 1, LANES * half : LANES * (half + 1)] = jnp.sum(item, axis=0, keepdims=True)
    middle = middle_of(moved[...])
    source_parts(rows[...], middle, feats, values)
    states = jnp.concatenate([moved[...], other[...]], axis=1) - middle
    sums[...] = pair_sums(states, feats, values, PART) + part[...]
    for q in range(CHIPS):
        here = slice(SLOTS * q, SLOTS * (q + 1))
        there = slice(COLS + SLOTS * q, COLS + SLOTS * (q + 1))
        for k in (2 * q, 2 * q + 1):
            fsend[k] = jnp.zeros((8, LANES), F32)
            fsend[k, :, 0:SLOTS] = sums[:, here]
            fsend[k, :, LISTED : LISTED + SLOTS] = sums[:, there]


def finish_kernel(keep, frecv, mine, place, slots, pos_o, vel_o, acc_o, jerk_o, fresh):
    total = frecv[0]
    for k in range(1, PLANE):
        total = total + frecv[k]
    once = mine[...]
    fresh[:, 0, :] = jnp.dot(once, slots[0], precision=EXACT, preferred_element_type=F32)[0:6]
    fresh[:, 1, :] = jnp.dot(total, slots[1], precision=EXACT, preferred_element_type=F32)[0:6]
    lane = iota((8, LANES), 1)
    spots = place[...]
    spread = [
        lax.dot_general(jnp.where(lane < RATES, value, 0.0), spots, NT, precision=EXACT, preferred_element_type=F32)
        for value in (once, total)
    ]
    lev = keep[12:13].astype(I32)
    stride = STEP_BASE * jnp.left_shift(jnp.ones_like(lev), lev).astype(F32)
    p, v, a, j = keep[0:3], keep[3:6], keep[6:9], keep[9:12]
    for step in range(2):
        new_a, new_j = spread[step][0:3], spread[step][3:6]
        hit = lev <= step
        p_new, v_new = correct(p, v, a, j, new_a, new_j, stride)
        p, v = jnp.where(hit, p_new, p), jnp.where(hit, v_new, v)
        a, j = jnp.where(hit, new_a, a), jnp.where(hit, new_j, j)
    pos_o[...] = p
    vel_o[...] = v
    acc_o[...] = a
    jerk_o[...] = j


def call(kernel, ins, outs, scratch=(), far=0, mib=8):
    vmem = pl.BlockSpec(memory_space=pltpu.VMEM)
    return pl.pallas_call(
        kernel,
        out_shape=[jax.ShapeDtypeStruct(s, F32) for s in outs],
        in_specs=[pl.BlockSpec(memory_space=pltpu.HBM)] * far + [vmem] * (len(ins) - far),
        out_specs=[vmem] * len(outs),
        scratch_shapes=list(scratch),
        compiler_params=pltpu.CompilerParams(vmem_limit_bytes=mib * 1024 * 1024),
    )(*ins)


def operands(sources):
    return [pltpu.VMEM((64, sources), BF16), pltpu.VMEM((32, sources), BF16)]


def gathered(value):
    for axes in STAGES:
        value = lax.all_gather(value, axes, tiled=True)
    return value.reshape(PLANE, 8, LANES)


def exchange(value, axes):
    return lax.all_to_all(value, axes, 0, 0, tiled=True)


def body(positions, velocities, accelerations, jerks, mass_weight, levels, active, counts):
    total_part = PART * lax.axis_size(ALL_AXES)
    lev = levels.reshape(1, PART)
    state = (positions, velocities, accelerations, jerks)

    def prepare(*refs):
        prepare_kernel(total_part, *refs)

    zsend, isend, place, slots, keep = call(
        prepare,
        (*state, mass_weight.reshape(1, PART), lev, active, counts.reshape(1, 2)),
        [(COLUMN, 16, PART), (8, LANES), (PART, LANES), (2, LANES, SLOTS), (16, PART)],
        [
            pltpu.VMEM((16, PART), F32),
            pltpu.VMEM((24, PART), F32),
            pltpu.VMEM((4, 3, PART), F32),
            pltpu.VMEM((1, PART), F32),
            pltpu.VMEM((1, PART), I32),
            pltpu.VMEM((2, SLOTS), I32),
            pltpu.VMEM((1, 2), I32),
            pltpu.SemaphoreType.DMA((8,)),
        ],
        far=8,
        mib=60,
    )
    irecv = gathered(isend)
    zrecv = exchange(zsend, "z")
    psend, known, other = call(
        first_kernel, (zrecv, irecv), [(PLANE, 2, 3 * COLS), (16, COLS), (8, COLS)], operands(COLUMN * PART), mib=24
    )
    precv = exchange(psend, PLANE_AXES)
    zsend2, moved, mine = call(update_kernel, (precv, known), [(COLUMN, 1, LANES), (8, COLS), (8, LANES)])
    zrecv2 = exchange(zsend2, "z")
    (part,) = call(later_kernel, (zrecv, moved, other), [(8, 2 * COLS)], operands(COLUMN * PART), mib=24)
    (fsend,) = call(
        last_kernel,
        (zrecv2, moved, other, part),
        [(PLANE, 8, LANES)],
        operands(PART) + [pltpu.VMEM((8, PART), F32), pltpu.VMEM((8, 2 * COLS), F32)],
    )
    frecv = exchange(fsend, PLANE_AXES)
    *state, fresh = call(
        finish_kernel,
        (keep, frecv, mine, place, slots),
        [(3, PART)] * 4 + [(6, 2, SLOTS)],
    )
    return (*state, fresh.transpose(1, 0, 2))


def solution(mesh):
    fine = Mesh(mesh.devices.reshape(2, 2, 2, 16, 2, 2), ALL_AXES)
    rows, flat = P(None, ALL_AXES), P(ALL_AXES)
    in_specs = (rows, rows, rows, rows, flat, flat, rows, rows)
    out_specs = (rows, rows, rows, rows, P(None, None, ALL_AXES))
    return jax.shard_map(body, mesh=fine, in_specs=in_specs, out_specs=out_specs, check_vma=False)
```

```python
import jax
import jax.numpy as jnp
from jax import lax
from jax.experimental import pallas as pl
from jax.experimental.pallas import tpu as pltpu
from jax.sharding import Mesh, PartitionSpec as P

STEP_BASE = 0.125
SOFTEN = 0.01
PART = 256
SLOTS = 24
CHIPS = 16
PLANE = 2 * CHIPS
COLUMN = 16
COLS = SLOTS * CHIPS
SHARE = SLOTS // 2
LANES = 128
LISTED = 32
RATES = 64
ALL_AXES = ("a", "b", "h", "z", "l", "c")
PLANE_AXES = ("a", "b", "h", "l", "c")
EXACT = lax.Precision.HIGHEST
F32 = jnp.float32
I32 = jnp.int32
BF16 = jnp.bfloat16
NT = (((1,), (1,)), ((), ()))
TN = (((0,), (0,)), ((), ()))


def predict(pos, vel, acc, jerk, elapsed):
    pred_pos = pos + elapsed * (vel + elapsed * (acc * 0.5 + elapsed * jerk / 6.0))
    pred_vel = vel + elapsed * (acc + elapsed * jerk * 0.5)
    return (pred_pos, pred_vel)


def correct(pos, vel, acc, jerk, new_acc, new_jerk, stride):
    half = 0.5 * stride
    square = stride * stride / 12.0
    vel_new = vel + half * (acc + new_acc) + square * (jerk - new_jerk)
    pos_new = pos + half * (vel + vel_new) + square * (acc - new_acc)
    return (pos_new, vel_new)


def iota(shape, axis):
    return lax.broadcasted_iota(I32, shape, axis)


def prepare_kernel(
    total, pos_h, vel_h, acc_h, jerk_h, weight_h, lev_h, active_h, counts_h, zsend, isend, place, slots, keep,
    srows, state, weight, levels, active, counts, sems,
):
    copies = [
        pltpu.make_async_copy(src, dst, sems.at[k])
        for k, (src, dst) in enumerate(
            (
                (pos_h, state.at[0]),
                (vel_h, state.at[1]),
                (acc_h, state.at[2]),
                (jerk_h, state.at[3]),
                (weight_h, weight),
                (lev_h, levels),
                (active_h, active),
                (counts_h, counts),
            )
        )
    ]
    for copy in copies:
        copy.start()
    for copy in copies:
        copy.wait()
    core = lax.axis_index("c")
    mass = weight[...] / total
    lev = levels[...]
    p, v, a, j = state[0], state[1], state[2], state[3]
    p1, v1 = predict(p, v, a, j, STEP_BASE)
    p2, v2 = predict(p, v, a, j, 2 * STEP_BASE)
    for k, part in enumerate((p, v, a, j)):
        keep[3 * k : 3 * k + 3] = part
    keep[12:13] = lev.astype(F32)
    keep[13:16] = jnp.zeros((3, PART), F32)
    later_mass = jnp.where(lev == 0, 0.0, mass)
    lines = [
        jnp.concatenate([part[k : k + 1] for part in (x, w) for k in range(3)] + [m], axis=1)
        for x, w, m in ((p1, v1, mass), (p2, v2, later_mass))
    ]
    both = jnp.concatenate(lines, axis=0)
    for k in range(COLUMN):
        zsend[k] = both
    srows[...] = jnp.zeros(srows.shape, F32)
    srows[0:3] = p
    srows[3:6] = v
    srows[6:7] = mass
    srows[8:11] = p2
    srows[11:14] = v2
    srows[16:19] = a
    srows[19:22] = j

    n1, n2 = counts[0:1, 0:1], counts[0:1, 1:2]
    off0 = jnp.where(core == 1, SLOTS - n1, 0)
    off1 = jnp.where(core == 1, n1, 0)
    who = iota((PART, SLOTS), 0)
    slot = iota((PART, SLOTS), 1)
    a1 = ((who == active[0:1, :]) & (slot < n1)).astype(F32)
    a2 = ((who == active[1:2, :]) & (slot < n2)).astype(F32)
    col = iota((LANES, SLOTS), 0)
    cslot = iota((LANES, SLOTS), 1)
    first = (col == cslot + off0) & (cslot < n1)
    again = (col == cslot + off0 + RATES) & (cslot < n1)
    first_f = first.astype(F32)
    listed = jnp.dot(jnp.broadcast_to(lev.astype(F32), (8, PART)), a2, preferred_element_type=F32)
    live = iota((8, SLOTS), 1) < n2
    is0 = (live & (listed < 0.5)).astype(F32)
    is1 = (live & (listed > 0.5) & (listed < 1.5)).astype(F32)
    before = (iota((SLOTS, SLOTS), 0) < iota((SLOTS, SLOTS), 1)).astype(F32)
    rank0 = jnp.dot(is0, before, preferred_element_type=F32)[0:1].astype(I32)
    rank1 = jnp.dot(is1, before, preferred_element_type=F32)[0:1].astype(I32)
    second = ((col == rank1 + (off1 + LISTED)) & (is1[0:1] > 0.5)).astype(F32)
    held = ((col == rank0 + off0) & (is0[0:1] > 0.5)).astype(F32)
    spots = lax.dot_general(a1, first_f + again.astype(F32), NT, preferred_element_type=F32)
    spots = spots + lax.dot_general(a2, second, NT, preferred_element_type=F32)
    place[...] = spots
    slots[0] = first_f
    slots[1] = held + second
    picked = jnp.dot(srows[...], spots, precision=EXACT, preferred_element_type=F32)
    lane = iota((8, LANES), 1)
    payload = jnp.where(lane < LISTED, picked[0:8], jnp.where(lane < RATES, picked[8:16], picked[16:24]))
    for k in range(PLANE):
        isend[k] = payload


def rounded(value):
    return value.astype(BF16).astype(F32)


def split(value):
    high = rounded(value)
    middle = rounded(value - high)
    return high, middle, value - high - middle


def middle_of(states):
    mean = jnp.sum(states, axis=1, keepdims=True) / states.shape[1]
    return jnp.where(iota(mean.shape, 0) < 6, mean, 0.0)


def source_parts(rows, middle, feats, values):
    count = rows.shape[0]
    rows = rows - jnp.concatenate([middle] * (count // 8), axis=0)
    row = iota(rows.shape, 0) % 8

    def ahead(value, by):
        return pltpu.roll(value, (count - by) % count, 0)

    square = rows * rows
    square = square + ahead(square, 1) + ahead(square, 2)
    cross = rows * ahead(rows, 3)
    cross = cross + ahead(cross, 1) + ahead(cross, 2)
    full = jnp.where(row == 6, 1.0, jnp.where(row == 7, ahead(square, count - 7), rows))
    high, middle, low = split(full)
    c_high, c_middle, c_low = split(cross)
    c_rows = jnp.where(row == 1, ahead(c_middle, count - 1), jnp.where(row == 2, ahead(c_low, count - 2), 0.0))
    c_rows = jnp.where(row == 0, c_high, c_rows)
    blank = jnp.zeros((8, PART), F32)
    for k in range(count // 8):
        here, cols = slice(8 * k, 8 * k + 8), slice(PART * k, PART * (k + 1))
        h, m, low_k = high[here], middle[here], low[here]
        feats[:, cols] = jnp.concatenate([h, h, m, m, h, low_k, c_rows[here], blank], axis=0).astype(BF16)
        weighed = rows[8 * k + 6 : 8 * k + 7] * jnp.where(row[here] == 6, 1.0, rows[here])
        weighed = jnp.where(row[here] == 7, 0.0, weighed)
        values[:, cols] = jnp.concatenate([*split(weighed), blank], axis=0).astype(BF16)


def target_parts(states):
    row = iota(states.shape, 0)
    square = states[0:3] * states[0:3]
    square = square[0:1] + square[1:2] + square[2:3] + SOFTEN
    cross = states[0:3] * states[3:6]
    cross = cross[0:1] + cross[1:2] + cross[2:3]
    turned = jnp.concatenate([states[3:6], states[0:3], states[6:8]], axis=0)
    near = jnp.where(row < 3, -2.0 * states, jnp.where(row < 6, 0.0, jnp.where(row == 6, square, 1.0)))
    rate = jnp.where(row < 6, -turned, jnp.where(row == 6, cross, 0.0))
    parts = []
    for full, one in ((near, 0.0), (rate, 1.0)):
        h, m, low = split(full)
        unit = jnp.where(row < 3, one, 0.0)
        parts.append(jnp.concatenate([h, m, h, m, low, h, unit, jnp.zeros_like(unit)], axis=0).astype(BF16))
    return parts


def pair_sums(states, feats, values, width):
    count = states.shape[1]
    both = jnp.concatenate(target_parts(states), axis=1)
    total = None
    for k in range(feats.shape[1] // width):
        cols = slice(width * k, width * (k + 1))
        product = lax.dot_general(feats[:, cols], both, TN, preferred_element_type=F32)
        inv = lax.rsqrt(jnp.maximum(product[:, :count], SOFTEN))
        inv2 = inv * inv
        w = inv * inv2
        terms = (w, w * inv2 * product[:, count:])
        high = [term.astype(BF16) for term in terms]
        low = [(term - part.astype(F32)).astype(BF16) for term, part in zip(terms, high)]
        for part in (high, low):
            term = jnp.dot(values[:, cols], jnp.concatenate(part, axis=1), preferred_element_type=F32)
            total = term if total is None else total + term
    sum_w, sum_u = total[:, :count], total[:, count:]
    w = sum_w[0:8] + sum_w[8:16] + sum_w[16:24]
    u = sum_u[0:8] + sum_u[8:16] + sum_u[16:24]
    acc = w[0:3] - states[0:3] * w[6:7]
    jerk = w[3:6] - states[3:6] * w[6:7] - 3.0 * (u[0:3] - states[0:3] * u[6:7])
    return jnp.concatenate([acc, jerk, jnp.zeros((2, states.shape[1]), F32)], axis=0)


def unpacked(zrecv, step, rows):
    rows[...] = jnp.zeros(rows.shape, F32)
    for k in range(7):
        for half in range(2):
            start = PART * k + LANES * half
            rows[half, pl.ds(k, COLUMN, stride=8), :] = zrecv[:, step, start : start + LANES]
    return jnp.concatenate([rows[0], rows[1]], axis=1)


def first_kernel(zrecv, irecv, psend, known, other, feats, values, rows):
    for q in range(CHIPS):
        block = irecv[2 * q] + irecv[2 * q + 1]
        here = slice(SLOTS * q, SLOTS * (q + 1))
        known[0:8, here] = block[:, 0:SLOTS]
        known[8:16, here] = block[:, RATES : RATES + SLOTS]
        other[:, here] = block[:, LISTED : LISTED + SLOTS]
    p1, v1 = predict(known[0:3], known[3:6], known[8:11], known[11:14], STEP_BASE)
    states = jnp.concatenate([p1, v1, jnp.zeros((2, COLS), F32)], axis=0)
    middle = middle_of(states)
    source_parts(unpacked(zrecv, 0, rows), middle, feats, values)
    part = pair_sums(states - middle, feats, values, 8 * PART)
    halves = [jnp.concatenate([part[3 * row + k : 3 * row + k + 1] for k in range(3)], axis=1) for row in range(2)]
    both = jnp.concatenate(halves, axis=0)
    for k in range(PLANE):
        psend[k] = both


def later_kernel(zrecv, moved, other, out, feats, values, rows):
    middle = middle_of(moved[...])
    source_parts(unpacked(zrecv, 1, rows), middle, feats, values)
    out[:, 0:COLS] = pair_sums(moved[...] - middle, feats, values, 8 * PART)
    out[:, COLS:] = pair_sums(other[...] - middle, feats, values, 8 * PART)


def update_kernel(precv, known, zsend, moved, mine):
    both = precv[0]
    for k in range(1, PLANE):
        both = both + precv[k]
    total = [both[row : row + 1, COLS * k : COLS * (k + 1)] for row in range(2) for k in range(3)]
    total = jnp.concatenate([*total, jnp.zeros((2, COLS), F32)], axis=0)
    p, v, a, j = known[0:3], known[3:6], known[8:11], known[11:14]
    new_a, new_j = total[0:3], total[3:6]
    pos, vel = correct(p, v, a, j, new_a, new_j, STEP_BASE)
    p2, v2 = predict(pos, vel, new_a, new_j, STEP_BASE)
    moved[0:3] = p2
    moved[3:6] = v2
    moved[6:7] = known[6:7]
    moved[7:8] = jnp.zeros((1, COLS), F32)
    chip = lax.axis_index("a")
    for axis in ("b", "h", "l"):
        chip = chip * 2 + lax.axis_index(axis)
    core = lax.axis_index("c")
    row = iota((COLS, LANES), 0)
    lane = iota((COLS, LANES), 1)
    index = lane % 16
    share = ((row == index + (chip * SLOTS + core * SHARE)) & (index < SHARE)).astype(F32)
    block = ((row == lane + chip * SLOTS) & (lane < SLOTS)).astype(F32)
    payload = jnp.dot(moved[...], share, precision=EXACT, preferred_element_type=F32)
    payload = jnp.where(iota((8, LANES), 0) == iota((8, LANES), 1) // 16, payload, 0.0)
    payload = jnp.sum(payload, axis=0, keepdims=True)
    for k in range(COLUMN):
        zsend[k] = payload
    mine[...] = jnp.dot(total, block, precision=EXACT, preferred_element_type=F32)


def last_kernel(zrecv, moved, other, part, fsend, feats, values, rows, sums):
    lane = iota((8, LANES), 1)
    rows[...] = jnp.zeros(rows.shape, F32)
    for half in range(2):
        packed = zrecv[8 * half : 8 * half + 8, 0, :]
        for k in range(7):
            item = jnp.where(lane < 16, pltpu.roll(packed, (LANES - 16 * k) % LANES, 1), 0.0)
            item = pltpu.roll(item, 0, 1, stride=16, stride_axis=0)
            rows[k : k + 1, LANES * half : LANES * (half + 1)] = jnp.sum(item, axis=0, keepdims=True)
    middle = middle_of(moved[...])
    source_parts(rows[...], middle, feats, values)
    states = jnp.concatenate([moved[...], other[...]], axis=1) - middle
    sums[...] = pair_sums(states, feats, values, PART) + part[...]
    for q in range(CHIPS):
        here = slice(SLOTS * q, SLOTS * (q + 1))
        there = slice(COLS + SLOTS * q, COLS + SLOTS * (q + 1))
        for k in (2 * q, 2 * q + 1):
            fsend[k] = jnp.zeros((8, LANES), F32)
            fsend[k, :, 0:SLOTS] = sums[:, here]
            fsend[k, :, LISTED : LISTED + SLOTS] = sums[:, there]


def finish_kernel(keep, frecv, mine, place, slots, pos_o, vel_o, acc_o, jerk_o, fresh):
    total = frecv[0]
    for k in range(1, PLANE):
        total = total + frecv[k]
    once = mine[...]
    fresh[:, 0, :] = jnp.dot(once, slots[0], precision=EXACT, preferred_element_type=F32)[0:6]
    fresh[:, 1, :] = jnp.dot(total, slots[1], precision=EXACT, preferred_element_type=F32)[0:6]
    lane = iota((8, LANES), 1)
    spots = place[...]
    spread = [
        lax.dot_general(jnp.where(lane < RATES, value, 0.0), spots, NT, precision=EXACT, preferred_element_type=F32)
        for value in (once, total)
    ]
    lev = keep[12:13].astype(I32)
    stride = STEP_BASE * jnp.left_shift(jnp.ones_like(lev), lev).astype(F32)
    p, v, a, j = keep[0:3], keep[3:6], keep[6:9], keep[9:12]
    for step in range(2):
        new_a, new_j = spread[step][0:3], spread[step][3:6]
        hit = lev <= step
        p_new, v_new = correct(p, v, a, j, new_a, new_j, stride)
        p, v = jnp.where(hit, p_new, p), jnp.where(hit, v_new, v)
        a, j = jnp.where(hit, new_a, a), jnp.where(hit, new_j, j)
    pos_o[...] = p
    vel_o[...] = v
    acc_o[...] = a
    jerk_o[...] = j


def call(kernel, ins, outs, scratch=(), far=0, mib=8):
    vmem = pl.BlockSpec(memory_space=pltpu.VMEM)
    return pl.pallas_call(
        kernel,
        out_shape=[jax.ShapeDtypeStruct(s, F32) for s in outs],
        in_specs=[pl.BlockSpec(memory_space=pltpu.HBM)] * far + [vmem] * (len(ins) - far),
        out_specs=[vmem] * len(outs),
        scratch_shapes=list(scratch),
        compiler_params=pltpu.CompilerParams(vmem_limit_bytes=mib * 1024 * 1024),
    )(*ins)


def operands(sources):
    return [pltpu.VMEM((64, sources), BF16), pltpu.VMEM((32, sources), BF16)]


def sources_scratch():
    return operands(COLUMN * PART) + [pltpu.VMEM((2, 8 * COLUMN, LANES), F32)]


def exchange(value, axes):
    return lax.all_to_all(value, axes, 0, 0, tiled=True)


def body(positions, velocities, accelerations, jerks, mass_weight, levels, active, counts):
    total_part = PART * lax.axis_size(ALL_AXES)
    lev = levels.reshape(1, PART)
    state = (positions, velocities, accelerations, jerks)

    def prepare(*refs):
        prepare_kernel(total_part, *refs)

    zsend, isend, place, slots, keep = call(
        prepare,
        (*state, mass_weight.reshape(1, PART), lev, active, counts.reshape(1, 2)),
        [(COLUMN, 2, 7 * PART), (PLANE, 8, LANES), (PART, LANES), (2, LANES, SLOTS), (16, PART)],
        [
            pltpu.VMEM((24, PART), F32),
            pltpu.VMEM((4, 3, PART), F32),
            pltpu.VMEM((1, PART), F32),
            pltpu.VMEM((1, PART), I32),
            pltpu.VMEM((2, SLOTS), I32),
            pltpu.VMEM((1, 2), I32),
            pltpu.SemaphoreType.DMA((8,)),
        ],
        far=8,
        mib=60,
    )
    irecv = exchange(isend, PLANE_AXES)
    zrecv = exchange(zsend, "z")
    psend, known, other = call(
        first_kernel, (zrecv, irecv), [(PLANE, 2, 3 * COLS), (16, COLS), (8, COLS)], sources_scratch(), mib=24
    )
    precv = exchange(psend, PLANE_AXES)
    zsend2, moved, mine = call(update_kernel, (precv, known), [(COLUMN, 1, LANES), (8, COLS), (8, LANES)])
    zrecv2 = exchange(zsend2, "z")
    (part,) = call(later_kernel, (zrecv, moved, other), [(8, 2 * COLS)], sources_scratch(), mib=24)
    (fsend,) = call(
        last_kernel,
        (zrecv2, moved, other, part),
        [(PLANE, 8, LANES)],
        operands(PART) + [pltpu.VMEM((8, PART), F32), pltpu.VMEM((8, 2 * COLS), F32)],
    )
    frecv = exchange(fsend, PLANE_AXES)
    *state, fresh = call(
        finish_kernel,
        (keep, frecv, mine, place, slots),
        [(3, PART)] * 4 + [(6, 2, SLOTS)],
    )
    return (*state, fresh.transpose(1, 0, 2))


def solution(mesh):
    fine = Mesh(mesh.devices.reshape(2, 2, 2, 16, 2, 2), ALL_AXES)
    rows, flat = P(None, ALL_AXES), P(ALL_AXES)
    in_specs = (rows, rows, rows, rows, flat, flat, rows, rows)
    out_specs = (rows, rows, rows, rows, P(None, None, ALL_AXES))
    return jax.shard_map(body, mesh=fine, in_specs=in_specs, out_specs=out_specs, check_vma=False)
```

```python
import jax
import jax.numpy as jnp
from jax import lax
from jax.experimental import pallas as pl
from jax.experimental.pallas import tpu as pltpu
from jax.sharding import Mesh, PartitionSpec as P

STEP_BASE = 0.125
SOFTEN = 0.01
PART = 256
SLOTS = 24
CHIPS = 16
PLANE = 2 * CHIPS
COLUMN = 16
COLS = SLOTS * CHIPS
SHARE = SLOTS // 2
LANES = 128
LISTED = 32
RATES = 64
ALL_AXES = ("a", "b", "h", "z", "l", "c")
PLANE_AXES = ("a", "b", "h", "l", "c")
STAGES = ("l", "h", "b", "a", "c")
EXACT = lax.Precision.HIGHEST
F32 = jnp.float32
I32 = jnp.int32
BF16 = jnp.bfloat16
NT = (((1,), (1,)), ((), ()))
TN = (((0,), (0,)), ((), ()))


def predict(pos, vel, acc, jerk, elapsed):
    pred_pos = pos + elapsed * (vel + elapsed * (acc * 0.5 + elapsed * jerk / 6.0))
    pred_vel = vel + elapsed * (acc + elapsed * jerk * 0.5)
    return (pred_pos, pred_vel)


def correct(pos, vel, acc, jerk, new_acc, new_jerk, stride):
    half = 0.5 * stride
    square = stride * stride / 12.0
    vel_new = vel + half * (acc + new_acc) + square * (jerk - new_jerk)
    pos_new = pos + half * (vel + vel_new) + square * (acc - new_acc)
    return (pos_new, vel_new)


def iota(shape, axis):
    return lax.broadcasted_iota(I32, shape, axis)


def prepare_kernel(
    total, pos_h, vel_h, acc_h, jerk_h, weight_h, lev_h, active_h, counts_h, zsend, isend, place, slots, keep,
    jrows, srows, state, weight, levels, active, counts, sems,
):
    copies = [
        pltpu.make_async_copy(src, dst, sems.at[k])
        for k, (src, dst) in enumerate(
            (
                (pos_h, state.at[0]),
                (vel_h, state.at[1]),
                (acc_h, state.at[2]),
                (jerk_h, state.at[3]),
                (weight_h, weight),
                (lev_h, levels),
                (active_h, active),
                (counts_h, counts),
            )
        )
    ]
    for copy in copies:
        copy.start()
    for copy in copies:
        copy.wait()
    core = lax.axis_index("c")
    mass = weight[...] / total
    lev = levels[...]
    p, v, a, j = state[0], state[1], state[2], state[3]
    p1, v1 = predict(p, v, a, j, STEP_BASE)
    p2, v2 = predict(p, v, a, j, 2 * STEP_BASE)
    for k, part in enumerate((p, v, a, j)):
        keep[3 * k : 3 * k + 3] = part
    keep[12:13] = lev.astype(F32)
    keep[13:16] = jnp.zeros((3, PART), F32)
    jrows[0:3] = p1
    jrows[3:6] = v1
    jrows[6:7] = mass
    jrows[7:8] = jnp.zeros((1, PART), F32)
    jrows[8:11] = p2
    jrows[11:14] = v2
    jrows[14:15] = jnp.where(lev == 0, 0.0, mass)
    jrows[15:16] = jnp.zeros((1, PART), F32)
    rows = jrows[...]
    for k in range(COLUMN):
        zsend[k] = rows
    srows[...] = jnp.zeros(srows.shape, F32)
    srows[0:3] = p
    srows[3:6] = v
    srows[6:7] = mass
    srows[8:11] = p2
    srows[11:14] = v2
    srows[16:19] = a
    srows[19:22] = j

    n1, n2 = counts[0:1, 0:1], counts[0:1, 1:2]
    off0 = jnp.where(core == 1, SLOTS - n1, 0)
    off1 = jnp.where(core == 1, n1, 0)
    who = iota((PART, SLOTS), 0)
    slot = iota((PART, SLOTS), 1)
    a1 = ((who == active[0:1, :]) & (slot < n1)).astype(F32)
    a2 = ((who == active[1:2, :]) & (slot < n2)).astype(F32)
    col = iota((LANES, SLOTS), 0)
    cslot = iota((LANES, SLOTS), 1)
    first = (col == cslot + off0) & (cslot < n1)
    again = (col == cslot + off0 + RATES) & (cslot < n1)
    first_f = first.astype(F32)
    listed = jnp.dot(jnp.broadcast_to(lev.astype(F32), (8, PART)), a2, preferred_element_type=F32)
    live = iota((8, SLOTS), 1) < n2
    is0 = (live & (listed < 0.5)).astype(F32)
    is1 = (live & (listed > 0.5) & (listed < 1.5)).astype(F32)
    before = (iota((SLOTS, SLOTS), 0) < iota((SLOTS, SLOTS), 1)).astype(F32)
    rank0 = jnp.dot(is0, before, preferred_element_type=F32)[0:1].astype(I32)
    rank1 = jnp.dot(is1, before, preferred_element_type=F32)[0:1].astype(I32)
    second = ((col == rank1 + (off1 + LISTED)) & (is1[0:1] > 0.5)).astype(F32)
    held = ((col == rank0 + off0) & (is0[0:1] > 0.5)).astype(F32)
    spots = lax.dot_general(a1, first_f + again.astype(F32), NT, preferred_element_type=F32)
    spots = spots + lax.dot_general(a2, second, NT, preferred_element_type=F32)
    place[...] = spots
    slots[0] = first_f
    slots[1] = held + second
    picked = jnp.dot(srows[...], spots, precision=EXACT, preferred_element_type=F32)
    lane = iota((8, LANES), 1)
    payload = jnp.where(lane < LISTED, picked[0:8], jnp.where(lane < RATES, picked[8:16], picked[16:24]))
    isend[...] = payload


def rounded(value):
    return value.astype(BF16).astype(F32)


def split(value):
    high = rounded(value)
    middle = rounded(value - high)
    return high, middle, value - high - middle


def middle_of(states):
    mean = jnp.sum(states, axis=1, keepdims=True) / states.shape[1]
    return jnp.where(iota(mean.shape, 0) < 6, mean, 0.0)


def source_parts(rows, middle, feats, values):
    count = rows.shape[0]
    rows = rows - jnp.concatenate([middle] * (count // 8), axis=0)
    row = iota(rows.shape, 0) % 8

    def ahead(value, by):
        return pltpu.roll(value, (count - by) % count, 0)

    square = rows * rows
    square = square + ahead(square, 1) + ahead(square, 2)
    cross = rows * ahead(rows, 3)
    cross = cross + ahead(cross, 1) + ahead(cross, 2)
    full = jnp.where(row == 6, 1.0, jnp.where(row == 7, ahead(square, count - 7), rows))
    high, middle, low = split(full)
    c_high, c_middle, c_low = split(cross)
    c_rows = jnp.where(row == 1, ahead(c_middle, count - 1), jnp.where(row == 2, ahead(c_low, count - 2), 0.0))
    c_rows = jnp.where(row == 0, c_high, c_rows)
    blank = jnp.zeros((8, PART), F32)
    for k in range(count // 8):
        here, cols = slice(8 * k, 8 * k + 8), slice(PART * k, PART * (k + 1))
        h, m, low_k = high[here], middle[here], low[here]
        feats[:, cols] = jnp.concatenate([h, h, m, m, h, low_k, c_rows[here], blank], axis=0).astype(BF16)
        weighed = rows[8 * k + 6 : 8 * k + 7] * jnp.where(row[here] == 6, 1.0, rows[here])
        weighed = jnp.where(row[here] == 7, 0.0, weighed)
        values[:, cols] = jnp.concatenate([*split(weighed), blank], axis=0).astype(BF16)


def target_parts(states):
    row = iota(states.shape, 0)
    square = states[0:3] * states[0:3]
    square = square[0:1] + square[1:2] + square[2:3] + SOFTEN
    cross = states[0:3] * states[3:6]
    cross = cross[0:1] + cross[1:2] + cross[2:3]
    turned = jnp.concatenate([states[3:6], states[0:3], states[6:8]], axis=0)
    near = jnp.where(row < 3, -2.0 * states, jnp.where(row < 6, 0.0, jnp.where(row == 6, square, 1.0)))
    rate = jnp.where(row < 6, -turned, jnp.where(row == 6, cross, 0.0))
    parts = []
    for full, one in ((near, 0.0), (rate, 1.0)):
        h, m, low = split(full)
        unit = jnp.where(row < 3, one, 0.0)
        parts.append(jnp.concatenate([h, m, h, m, low, h, unit, jnp.zeros_like(unit)], axis=0).astype(BF16))
    return parts


def pair_sums(states, feats, values, width):
    count = states.shape[1]
    both = jnp.concatenate(target_parts(states), axis=1)
    total = None
    for k in range(feats.shape[1] // width):
        cols = slice(width * k, width * (k + 1))
        product = lax.dot_general(feats[:, cols], both, TN, preferred_element_type=F32)
        inv = lax.rsqrt(jnp.maximum(product[:, :count], SOFTEN))
        inv2 = inv * inv
        w = inv * inv2
        terms = (w, w * inv2 * product[:, count:])
        high = [term.astype(BF16) for term in terms]
        low = [(term - part.astype(F32)).astype(BF16) for term, part in zip(terms, high)]
        for part in (high, low):
            term = jnp.dot(values[:, cols], jnp.concatenate(part, axis=1), preferred_element_type=F32)
            total = term if total is None else total + term
    sum_w, sum_u = total[:, :count], total[:, count:]
    w = sum_w[0:8] + sum_w[8:16] + sum_w[16:24]
    u = sum_u[0:8] + sum_u[8:16] + sum_u[16:24]
    acc = w[0:3] - states[0:3] * w[6:7]
    jerk = w[3:6] - states[3:6] * w[6:7] - 3.0 * (u[0:3] - states[0:3] * u[6:7])
    return jnp.concatenate([acc, jerk, jnp.zeros((2, states.shape[1]), F32)], axis=0)


def first_kernel(zrecv, irecv, psend, known, other, feats, values):
    for q in range(CHIPS):
        block = irecv[q] + irecv[CHIPS + q]
        here = slice(SLOTS * q, SLOTS * (q + 1))
        known[0:8, here] = block[:, 0:SLOTS]
        known[8:16, here] = block[:, RATES : RATES + SLOTS]
        other[:, here] = block[:, LISTED : LISTED + SLOTS]
    p1, v1 = predict(known[0:3], known[3:6], known[8:11], known[11:14], STEP_BASE)
    states = jnp.concatenate([p1, v1, jnp.zeros((2, COLS), F32)], axis=0)
    middle = middle_of(states)
    source_parts(zrecv[:, 0:8, :].reshape(8 * COLUMN, PART), middle, feats, values)
    part = pair_sums(states - middle, feats, values, 8 * PART)
    halves = [jnp.concatenate([part[3 * row + k : 3 * row + k + 1] for k in range(3)], axis=1) for row in range(2)]
    both = jnp.concatenate(halves, axis=0)
    for k in range(PLANE):
        psend[k] = both


def later_kernel(zrecv, moved, other, out, feats, values):
    middle = middle_of(moved[...])
    source_parts(zrecv[:, 8:16, :].reshape(8 * COLUMN, PART), middle, feats, values)
    out[:, 0:COLS] = pair_sums(moved[...] - middle, feats, values, 8 * PART)
    out[:, COLS:] = pair_sums(other[...] - middle, feats, values, 8 * PART)


def update_kernel(precv, known, zsend, moved, mine):
    both = precv[0]
    for k in range(1, PLANE):
        both = both + precv[k]
    total = [both[row : row + 1, COLS * k : COLS * (k + 1)] for row in range(2) for k in range(3)]
    total = jnp.concatenate([*total, jnp.zeros((2, COLS), F32)], axis=0)
    p, v, a, j = known[0:3], known[3:6], known[8:11], known[11:14]
    new_a, new_j = total[0:3], total[3:6]
    pos, vel = correct(p, v, a, j, new_a, new_j, STEP_BASE)
    p2, v2 = predict(pos, vel, new_a, new_j, STEP_BASE)
    moved[0:3] = p2
    moved[3:6] = v2
    moved[6:7] = known[6:7]
    moved[7:8] = jnp.zeros((1, COLS), F32)
    chip = lax.axis_index("a")
    for axis in ("b", "h", "l"):
        chip = chip * 2 + lax.axis_index(axis)
    core = lax.axis_index("c")
    row = iota((COLS, LANES), 0)
    lane = iota((COLS, LANES), 1)
    index = lane % 16
    share = ((row == index + (chip * SLOTS + core * SHARE)) & (index < SHARE)).astype(F32)
    block = ((row == lane + chip * SLOTS) & (lane < SLOTS)).astype(F32)
    payload = jnp.dot(moved[...], share, precision=EXACT, preferred_element_type=F32)
    payload = jnp.where(iota((8, LANES), 0) == iota((8, LANES), 1) // 16, payload, 0.0)
    payload = jnp.sum(payload, axis=0, keepdims=True)
    for k in range(COLUMN):
        zsend[k] = payload
    mine[...] = jnp.dot(total, block, precision=EXACT, preferred_element_type=F32)


def last_kernel(zrecv, moved, other, part, fsend, feats, values, rows, sums):
    lane = iota((8, LANES), 1)
    rows[...] = jnp.zeros(rows.shape, F32)
    for half in range(2):
        packed = zrecv[8 * half : 8 * half + 8, 0, :]
        for k in range(7):
            item = jnp.where(lane < 16, pltpu.roll(packed, (LANES - 16 * k) % LANES, 1), 0.0)
            item = pltpu.roll(item, 0, 1, stride=16, stride_axis=0)
            rows[k : k + 1, LANES * half : LANES * (half + 1)] = jnp.sum(item, axis=0, keepdims=True)
    middle = middle_of(moved[...])
    source_parts(rows[...], middle, feats, values)
    states = jnp.concatenate([moved[...], other[...]], axis=1) - middle
    sums[...] = pair_sums(states, feats, values, PART) + part[...]
    for q in range(CHIPS):
        here = slice(SLOTS * q, SLOTS * (q + 1))
        there = slice(COLS + SLOTS * q, COLS + SLOTS * (q + 1))
        for k in (2 * q, 2 * q + 1):
            fsend[k] = jnp.zeros((8, LANES), F32)
            fsend[k, :, 0:SLOTS] = sums[:, here]
            fsend[k, :, LISTED : LISTED + SLOTS] = sums[:, there]


def finish_kernel(keep, frecv, mine, place, slots, pos_o, vel_o, acc_o, jerk_o, fresh):
    total = frecv[0]
    for k in range(1, PLANE):
        total = total + frecv[k]
    once = mine[...]
    fresh[:, 0, :] = jnp.dot(once, slots[0], precision=EXACT, preferred_element_type=F32)[0:6]
    fresh[:, 1, :] = jnp.dot(total, slots[1], precision=EXACT, preferred_element_type=F32)[0:6]
    lane = iota((8, LANES), 1)
    spots = place[...]
    spread = [
        lax.dot_general(jnp.where(lane < RATES, value, 0.0), spots, NT, precision=EXACT, preferred_element_type=F32)
        for value in (once, total)
    ]
    lev = keep[12:13].astype(I32)
    stride = STEP_BASE * jnp.left_shift(jnp.ones_like(lev), lev).astype(F32)
    p, v, a, j = keep[0:3], keep[3:6], keep[6:9], keep[9:12]
    for step in range(2):
        new_a, new_j = spread[step][0:3], spread[step][3:6]
        hit = lev <= step
        p_new, v_new = correct(p, v, a, j, new_a, new_j, stride)
        p, v = jnp.where(hit, p_new, p), jnp.where(hit, v_new, v)
        a, j = jnp.where(hit, new_a, a), jnp.where(hit, new_j, j)
    pos_o[...] = p
    vel_o[...] = v
    acc_o[...] = a
    jerk_o[...] = j


def call(kernel, ins, outs, scratch=(), far=0, mib=8):
    vmem = pl.BlockSpec(memory_space=pltpu.VMEM)
    return pl.pallas_call(
        kernel,
        out_shape=[jax.ShapeDtypeStruct(s, F32) for s in outs],
        in_specs=[pl.BlockSpec(memory_space=pltpu.HBM)] * far + [vmem] * (len(ins) - far),
        out_specs=[vmem] * len(outs),
        scratch_shapes=list(scratch),
        compiler_params=pltpu.CompilerParams(vmem_limit_bytes=mib * 1024 * 1024),
    )(*ins)


def operands(sources):
    return [pltpu.VMEM((64, sources), BF16), pltpu.VMEM((32, sources), BF16)]


def gathered(value):
    for axes in STAGES:
        value = lax.all_gather(value, axes, tiled=True)
    return value.reshape(PLANE, 8, LANES)


def exchange(value, axes):
    return lax.all_to_all(value, axes, 0, 0, tiled=True)


def body(positions, velocities, accelerations, jerks, mass_weight, levels, active, counts):
    total_part = PART * lax.axis_size(ALL_AXES)
    lev = levels.reshape(1, PART)
    state = (positions, velocities, accelerations, jerks)

    def prepare(*refs):
        prepare_kernel(total_part, *refs)

    zsend, isend, place, slots, keep = call(
        prepare,
        (*state, mass_weight.reshape(1, PART), lev, active, counts.reshape(1, 2)),
        [(COLUMN, 16, PART), (8, LANES), (PART, LANES), (2, LANES, SLOTS), (16, PART)],
        [
            pltpu.VMEM((16, PART), F32),
            pltpu.VMEM((24, PART), F32),
            pltpu.VMEM((4, 3, PART), F32),
            pltpu.VMEM((1, PART), F32),
            pltpu.VMEM((1, PART), I32),
            pltpu.VMEM((2, SLOTS), I32),
            pltpu.VMEM((1, 2), I32),
            pltpu.SemaphoreType.DMA((8,)),
        ],
        far=8,
        mib=60,
    )
    irecv = gathered(isend)
    zrecv = exchange(zsend, "z")
    psend, known, other = call(
        first_kernel, (zrecv, irecv), [(PLANE, 2, 3 * COLS), (16, COLS), (8, COLS)], operands(COLUMN * PART), mib=24
    )
    precv = exchange(psend, PLANE_AXES)
    zsend2, moved, mine = call(update_kernel, (precv, known), [(COLUMN, 1, LANES), (8, COLS), (8, LANES)])
    zrecv2 = exchange(zsend2, "z")
    (part,) = call(later_kernel, (zrecv, moved, other), [(8, 2 * COLS)], operands(COLUMN * PART), mib=24)
    (fsend,) = call(
        last_kernel,
        (zrecv2, moved, other, part),
        [(PLANE, 8, LANES)],
        operands(PART) + [pltpu.VMEM((8, PART), F32), pltpu.VMEM((8, 2 * COLS), F32)],
    )
    frecv = exchange(fsend, PLANE_AXES)
    *state, fresh = call(
        finish_kernel,
        (keep, frecv, mine, place, slots),
        [(3, PART)] * 4 + [(6, 2, SLOTS)],
    )
    return (*state, fresh.transpose(1, 0, 2))


def solution(mesh):
    fine = Mesh(mesh.devices.reshape(2, 2, 2, 16, 2, 2), ALL_AXES)
    rows, flat = P(None, ALL_AXES), P(ALL_AXES)
    in_specs = (rows, rows, rows, rows, flat, flat, rows, rows)
    out_specs = (rows, rows, rows, rows, P(None, None, ALL_AXES))
    return jax.shard_map(body, mesh=fine, in_specs=in_specs, out_specs=out_specs, check_vma=False)
```
